1024 devices in a mesh: dom: 64 (over z, y_lo, core), rows: 16 (over x, y_hi).
Axes of the slice: x: 4, y: 8 (y_hi: 4, y_lo: 2; y = y_hi * 2 + y_lo), z: 16, core: 2. Of those that a mesh axis runs over, the one named last changes fastest.
Arguments:
- features: bfloat16 [524288, 256], P(('dom', 'rows')), may hold values from -6 to 6
- weight: bfloat16 [256, 256], replicated, may hold values from -0.375 to 0.375
- tile_values: bfloat16 [1024, 5, 4, 128, 128], P(('dom', 'rows')), may hold values from -0.1875 to 0.1875
- tile_source: int32 [1024, 5, 4], P(('dom', 'rows')), may hold values from 0 to 3
- tile_slot: int32 [1024, 5, 4], P(('dom', 'rows')), may hold values from 0 to 31
- slot_block: int32 [1024, 32], P(('dom', 'rows')), may hold values from 0 to 3
- tile_count: int32 [1024, 5], P(('dom', 'rows')), may hold values from 1 to 4
- cotangent: bfloat16 [524288, 256], P(('dom', 'rows')), may hold values from -6 to 6
Outputs:
- activations: bfloat16 [524288, 256], P(('dom', 'rows'))
- feature_grad: bfloat16 [524288, 256], P(('dom', 'rows'))
- weight_grad: float32 [256, 256], replicated
The draws below stay inside these ranges and needn't reach their ends.
Inputs may be any that keep to these rules, and one draw needn't show every extreme that they name: Tiles of index tile_count[g, k] and above at offset index k are padding; their tile_values, tile_source and tile_slot count for nothing.
All inputs are finite; a program needn't handle non-finite values.
Results may differ from the reference program's by a relative error of at most 0.019.
Values may be sent and summed in bfloat16 or wider, within the bound.
No kernel may reach another device: no remote copies, remote signals or barrier semaphores. Data moves between devices by JAX's collectives and lax.ppermute only.
A program may use at most 32 MiB of HBM per device.

```python
import jax
import jax.numpy as jnp
from jax import lax

F = 256
BLOCK = 128
BLK_DEV = 4
HALF = 2
TPS = 4
CAP = 2
STEPS = 5
NODES = 524288
N_DOM = 64
N_ROWS = 16
DEVICES = 1024


def set_ends(drawn, own_key, least, largest):
    spot = [jax.random.randint(jax.random.fold_in(own_key, axis), (), 0, length) for axis, length in enumerate(drawn.shape)]
    main_axis = drawn.shape.index(max(drawn.shape))
    beside = spot[:main_axis] + [(spot[main_axis] + 1) % drawn.shape[main_axis]] + spot[main_axis + 1:]
    return drawn.at[tuple(spot)].set(least).at[tuple(beside)].set(largest)


def levels(rng, dims, split, least, high):
    level, own = 1.0, jax.random.fold_in(rng, 6)
    for dim, shards_of in split:
        draws = jnp.exp(jax.random.uniform(jax.random.fold_in(own, dim), (shards_of,), jnp.float32, least / len(split), high / len(split)))
        level = level * jnp.repeat(draws, dims[dim] // shards_of).reshape([-1 if axis == dim else 1 for axis in range(len(dims))])
    return level


def centred(own_key, shape, spread, most, split=(), kind=jnp.bfloat16):
    array = jax.random.normal(own_key, shape, jnp.float32) * spread
    if len(split) > 0:
        array = levels(own_key, shape, split, -0.22, 0.18) * array
    return jnp.clip(array, min=-most, max=most).astype(kind)


def setup_inputs(seed: int = 0) -> dict:
    key_of = jax.random.split(jax.random.key(seed), 9)
    features = centred(key_of[0], (NODES, F), 1.0, 6.0, ((0, 1024),))
    weight = centred(key_of[1], (F, F), F ** -0.5, 0.375)
    tile_values = centred(key_of[2], (DEVICES, STEPS, TPS, BLOCK, BLOCK), (BLOCK * 8) ** -0.5, 0.1875, ((0, 1024),))
    tile_source = set_ends(jax.random.randint(key_of[3], (DEVICES, STEPS, TPS), 0, BLK_DEV), jax.random.fold_in(key_of[3], 1), 0, BLK_DEV - 1).astype(jnp.int32)
    tile_slot = set_ends(jax.random.randint(key_of[4], (DEVICES, STEPS, TPS), 0, N_ROWS * CAP), jax.random.fold_in(key_of[4], 1), 0, (N_ROWS * CAP) - 1).astype(jnp.int32)
    slot_block = set_ends(jax.random.randint(key_of[5], (DEVICES, N_ROWS * CAP), 0, BLK_DEV), jax.random.fold_in(key_of[5], 1), 0, BLK_DEV - 1).astype(jnp.int32)
    tile_count = set_ends(jax.random.randint(key_of[6], (DEVICES, STEPS), 1, TPS + 1), jax.random.fold_in(key_of[6], 1), 1, TPS).astype(jnp.int32)
    cotangent = centred(key_of[7], (NODES, F), 1.0, 6.0, ((0, 1024),))
    return {"features": features, "weight": weight, "tile_values": tile_values, "tile_source": tile_source, "tile_slot": tile_slot, "slot_block": slot_block, "tile_count": tile_count, "cotangent": cotangent}


def reference(features, weight, tile_values, tile_source, tile_slot, slot_block, tile_count, cotangent):
    channels = features.shape[1]
    slot_total = N_ROWS * CAP
    blocks = features.reshape(-1, BLOCK, channels)
    values = tile_values.reshape(N_DOM, N_ROWS, STEPS, TPS, BLOCK, BLOCK)
    sources = tile_source.reshape(N_DOM, N_ROWS, STEPS, TPS)
    slot_ids = tile_slot.reshape(N_DOM, N_ROWS, STEPS, TPS)
    targets = slot_block.reshape(N_DOM, N_ROWS, slot_total)
    counts = tile_count.reshape(N_DOM, N_ROWS, STEPS)
    offsets = jnp.arange(STEPS, dtype=jnp.int32) - HALF
    row_ids = jnp.arange(N_ROWS, dtype=jnp.int32)
    tile_ids = jnp.arange(TPS, dtype=jnp.int32)
    slot_owner = jnp.arange(slot_total, dtype=jnp.int32) // CAP

    def layout(dom_index):
        src_dev = ((dom_index + offsets)[None, :] % N_DOM) * N_ROWS + row_ids[:, None]
        src_glob = src_dev[:, :, None] * BLK_DEV + sources[dom_index]
        live_mask = (tile_ids[None, None, :] < counts[dom_index][:, :, None]).astype(jnp.float32)
        flat_slots = slot_ids[dom_index].reshape(N_ROWS, STEPS * TPS)
        tile_target = jnp.take_along_axis(targets[dom_index], flat_slots, axis=1).reshape(N_ROWS, STEPS, TPS)
        dest_local = (slot_ids[dom_index] // CAP) * BLK_DEV + tile_target
        return src_glob.astype(jnp.int32), live_mask, dest_local.astype(jnp.int32)

    def forward_dom(dom_index):
        src_glob, live_mask, dest_local = layout(dom_index)
        picked = blocks[src_glob].astype(jnp.float32)
        product = jnp.einsum("rstij,rstjf->rstif", values[dom_index].astype(jnp.float32), picked)
        product = product * live_mask[..., None, None]
        segment_ids = row_ids[:, None, None] * slot_total + slot_ids[dom_index]
        partial_value = jax.ops.segment_sum(product.reshape(-1, BLOCK, channels), segment_ids.reshape(-1),
                                      num_segments=N_ROWS * slot_total).astype(jnp.bfloat16)
        slot_dest = slot_owner[None, :] * BLK_DEV + targets[dom_index]
        summed = jax.ops.segment_sum(partial_value.astype(jnp.float32), slot_dest.reshape(-1),
                                     num_segments=N_ROWS * BLK_DEV)
        return summed.astype(jnp.bfloat16)

    aggregate = lax.map(forward_dom, jnp.arange(N_DOM, dtype=jnp.int32)).reshape(-1, channels)
    pre_act = jnp.dot(aggregate, weight, preferred_element_type=jnp.float32)
    activations = jax.nn.silu(pre_act).astype(jnp.bfloat16)
    sigmoid_pre = jax.nn.sigmoid(pre_act)
    slope_factor = sigmoid_pre * (1.0 + pre_act * (1.0 - sigmoid_pre))
    pre_grad = (cotangent.astype(jnp.float32) * slope_factor).astype(jnp.bfloat16)
    weight_grad = jnp.dot(aggregate.T, pre_grad, preferred_element_type=jnp.float32)
    agg_grad = jnp.dot(pre_grad, weight.T, preferred_element_type=jnp.float32).astype(jnp.bfloat16)
    grad_blocks = agg_grad.reshape(-1, BLOCK, channels)

    def backward_dom(source_grad, dom_index):
        src_glob, live_mask, dest_local = layout(dom_index)
        picked = grad_blocks[dom_index * N_ROWS * BLK_DEV + dest_local].astype(jnp.float32)
        product = jnp.einsum("rstji,rstjf->rstif", values[dom_index].astype(jnp.float32), picked)
        product = product * live_mask[..., None, None]
        source_grad = source_grad.at[src_glob.reshape(-1)].add(product.reshape(-1, BLOCK, channels))
        return source_grad, None

    start_grad = jnp.zeros((blocks.shape[0], BLOCK, channels), jnp.float32)
    source_grad = lax.scan(backward_dom, start_grad, jnp.arange(N_DOM, dtype=jnp.int32))[0]
    feature_grad = source_grad.reshape(-1, channels).astype(jnp.bfloat16)
    return activations, feature_grad, weight_grad
```

```python
import functools

import jax
import jax.numpy as jnp
from jax import lax
from jax.experimental import pallas as pl
from jax.experimental.pallas import tpu as pltpu
from jax.sharding import PartitionSpec as P

BLOCK = 128
HALF = 2
CAP = 2
XN = 4
YN = 4
LANES = 128
ID_ROWS = 16

OFFSETS = (-2, -1, 1, 2)
VMEM = pl.BlockSpec(memory_space=pltpu.VMEM)
SMEM = pl.BlockSpec(memory_space=pltpu.SMEM)
BF16 = jnp.bfloat16
F32 = jnp.float32


def params():
    return pltpu.CompilerParams(vmem_limit_bytes=24 * 1024 * 1024)


def cost(flops, nbytes):
    return pl.CostEstimate(flops=flops, bytes_accessed=nbytes, transcendentals=0)


def dom_shift(value, steps):
    count = lax.axis_size("dom")
    return lax.ppermute(value, "dom", [(i, (i + steps) % count) for i in range(count)])


def y_shift(value, steps):
    pairs = [(x * YN + y, x * YN + (y + steps) % YN) for x in range(XN) for y in range(YN)]
    return lax.ppermute(value, "rows", pairs)


X_GROUPS = [[x * YN + y for x in range(XN)] for y in range(YN)]


def x_exchange(value):
    return lax.all_to_all(
        value, "rows", split_axis=0, concat_axis=0, tiled=True, axis_index_groups=X_GROUPS
    )


def grouped_sum(value, axis, groups):
    size = len(groups[0])
    spread = jnp.broadcast_to(value[None], (size,) + value.shape)
    return jnp.sum(
        lax.all_to_all(
            spread, axis, split_axis=0, concat_axis=0, tiled=True, axis_index_groups=groups
        ),
        axis=0,
    )


def forward_kernel(with_ids, src, slot, cnt, fm2, fm1, f0, fp1, fp2, vals, ids, out, acc):
    acc[...] = jnp.zeros_like(acc)
    feats = (fm2, fm1, f0, fp1, fp2)
    tiles_step = vals.shape[0] // len(feats)
    for k, feat in enumerate(feats):
        for t in range(tiles_step):
            n = k * tiles_step + t

            @pl.when(t < cnt[0, k])
            def _():
                block = feat[src[k, t]]
                acc[slot[k, t]] += jnp.dot(vals[n], block, preferred_element_type=F32)

    per_x = acc.shape[0] // XN
    for s in range(acc.shape[0]):
        out[s // per_x, pl.ds((s % per_x) * BLOCK, BLOCK), :] = acc[s].astype(BF16)
    if with_ids:
        for x in range(XN):
            out[x, pl.ds(per_x * BLOCK, ID_ROWS), :] = ids[x]


def forward_products(src, slot, cnt, feats, vals, ids, with_ids):
    slots = XN * YN * CAP
    rows = YN * CAP * BLOCK + (ID_ROWS if with_ids else 0)
    return pl.pallas_call(
        functools.partial(forward_kernel, with_ids),
        out_shape=jax.ShapeDtypeStruct((XN, rows, LANES), BF16),
        in_specs=[SMEM] * 3 + [VMEM] * 7,
        out_specs=VMEM,
        scratch_shapes=[pltpu.VMEM((slots, BLOCK, LANES), F32)],
        compiler_params=params(),
        cost_estimate=cost(vals.shape[0] * 2 * BLOCK * BLOCK * LANES, 4 << 20),
        name="tile_forward",
    )(src, slot, cnt, *feats, vals, ids)


def gather_kernel(blocks_dev, recv, ids, out):
    for y in range(YN):
        for b in range(blocks_dev):
            total = jnp.zeros((BLOCK, LANES), F32)
            for x in range(XN):
                for c in range(CAP):
                    j = y * CAP + c
                    hit = ids[pl.ds(x * 8 + j, 1), :] == float(b)
                    part = recv[x, pl.ds(j * BLOCK, BLOCK), :].astype(F32)
                    total = total + jnp.where(hit, part, 0.0)
            out[y, pl.ds(b * BLOCK, BLOCK), :] = total.astype(BF16)


def gather_blocks(recv, ids, blocks_dev):
    return pl.pallas_call(
        functools.partial(gather_kernel, blocks_dev),
        out_shape=jax.ShapeDtypeStruct((YN, blocks_dev * BLOCK, LANES), BF16),
        in_specs=[VMEM, VMEM],
        out_specs=VMEM,
        compiler_params=params(),
        cost_estimate=cost(1 << 20, 2 << 20),
        name="block_sums",
    )(recv, ids)


def dense_kernel(*refs):
    own = refs[0:2]
    far = refs[2:8]
    me, weight, cot, act, g0, g1, wgrad = refs[8:]
    y = me[0]
    halves = []
    for h in range(2):
        total = own[h][y].astype(F32)
        for k in range(3):
            total = total + far[h * 3 + k][...].astype(F32)
        halves.append(total.astype(BF16))
    agg = jnp.concatenate(halves, axis=1)
    w = weight[...]
    pre = jnp.dot(agg, w, preferred_element_type=F32)
    sig = 1.0 / (1.0 + jnp.exp(-pre))
    act[...] = (pre * sig).astype(BF16)
    slope = sig * (1.0 + pre * (1.0 - sig))
    pre_grad = (cot[...].astype(F32) * slope).astype(BF16)
    grad = lax.dot_general(
        pre_grad, w, (((1,), (1,)), ((), ())), preferred_element_type=F32
    ).astype(BF16)
    g0[...] = grad[:, :LANES]
    g1[...] = grad[:, LANES:]
    wgrad[...] = lax.dot_general(
        agg, pre_grad, (((0,), (0,)), ((), ())), preferred_element_type=F32
    )


def dense(own, far, me, weight, cot):
    nodes, channels = cot.shape
    return pl.pallas_call(
        dense_kernel,
        out_shape=(
            jax.ShapeDtypeStruct((nodes, channels), BF16),
            jax.ShapeDtypeStruct((nodes, LANES), BF16),
            jax.ShapeDtypeStruct((nodes, LANES), BF16),
            jax.ShapeDtypeStruct((channels, channels), F32),
        ),
        in_specs=[VMEM] * 8 + [SMEM] + [VMEM] * 2,
        out_specs=(VMEM,) * 4,
        compiler_params=params(),
        cost_estimate=cost(6 * nodes * channels * channels, 4 << 20),
        name="dense_layer",
    )(*own, *far, me, weight, cot)


def reply_kernel(blocks_dev, me, g0, g1, g2, g3, ids, out):
    for k, grads in enumerate((g0, g1, g2, g3)):
        y = lax.rem(me[0] - k + YN, YN)
        blocks = [grads[pl.ds(b * BLOCK, BLOCK), :].astype(F32) for b in range(blocks_dev)]
        for x in range(XN):
            for c in range(CAP):
                j = y * CAP + c
                row = ids[pl.ds(x * 8 + j, 1), :]
                picked = jnp.where(row == 0.0, blocks[0], 0.0)
                for b in range(1, blocks_dev):
                    picked = jnp.where(row == float(b), blocks[b], picked)
                start = pl.multiple_of(j * BLOCK, BLOCK)
                out[x, pl.ds(start, BLOCK), :] = picked.astype(BF16)


def reply_blocks(me, grads, ids, blocks_dev):
    return pl.pallas_call(
        functools.partial(reply_kernel, blocks_dev),
        out_shape=jax.ShapeDtypeStruct((XN, YN * CAP * BLOCK, LANES), BF16),
        in_specs=[SMEM] + [VMEM] * 5,
        out_specs=VMEM,
        compiler_params=params(),
        cost_estimate=cost(1 << 20, 2 << 20),
        name="slot_replies",
    )(me, *grads, ids)


def backward_kernel(src, slot, cnt, ret, vals, om2, om1, o0, op1, op2, acc):
    outs = (om2, om1, o0, op1, op2)
    tiles_step = vals.shape[0] // len(outs)
    per_x = ret.shape[1] // BLOCK
    for k, out in enumerate(outs):
        acc[...] = jnp.zeros_like(acc)
        for t in range(tiles_step):
            n = k * tiles_step + t

            @pl.when(t < cnt[0, k])
            def _():
                s = slot[k, t]
                start = pl.multiple_of((s % per_x) * BLOCK, BLOCK)
                block = ret[s // per_x, pl.ds(start, BLOCK), :]
                acc[src[k, t]] += lax.dot_general(
                    vals[n], block, (((0,), (0,)), ((), ())), preferred_element_type=F32
                )

        for b in range(acc.shape[0]):
            out[pl.ds(b * BLOCK, BLOCK), :] = acc[b].astype(out.dtype)


def backward_products(src, slot, cnt, ret, vals, blocks_dev):
    half = jax.ShapeDtypeStruct((blocks_dev * BLOCK, LANES), BF16)
    full = jax.ShapeDtypeStruct((blocks_dev * BLOCK, LANES), F32)
    return pl.pallas_call(
        backward_kernel,
        out_shape=(half, half, full, half, half),
        in_specs=[SMEM] * 3 + [VMEM] * 2,
        out_specs=(VMEM,) * 5,
        scratch_shapes=[pltpu.VMEM((blocks_dev, BLOCK, LANES), F32)],
        compiler_params=params(),
        cost_estimate=cost(vals.shape[0] * 2 * BLOCK * BLOCK * LANES, 4 << 20),
        name="tile_backward",
    )(src, slot, cnt, ret, vals)


def final_kernel(*refs):
    out = refs[-1]
    for h in range(2):
        total = refs[h * 5][...]
        for k in range(1, 5):
            total = total + refs[h * 5 + k][...].astype(F32)
        out[:, h * LANES : (h + 1) * LANES] = total.astype(BF16)


def final_sum(parts):
    nodes = parts[0].shape[0]
    return pl.pallas_call(
        final_kernel,
        out_shape=jax.ShapeDtypeStruct((nodes, 2 * LANES), BF16),
        in_specs=[VMEM] * len(parts),
        out_specs=VMEM,
        compiler_params=params(),
        cost_estimate=cost(1 << 20, 2 << 20),
        name="grad_sum",
    )(*parts)


def per_device(
    features, weight, tile_values, tile_source, tile_slot, slot_block, tile_count, cotangent
):
    blocks_dev = features.shape[0] // BLOCK
    dom_count = lax.axis_size("dom")
    vals = tile_values.reshape(-1, BLOCK, BLOCK)
    src, slot, cnt = tile_source[0], tile_slot[0], tile_count
    me = (lax.axis_index("rows") % YN).astype(jnp.int32).reshape(1)
    id_rows = jnp.broadcast_to(
        jnp.pad(slot_block.reshape(XN, -1), ((0, 0), (0, ID_ROWS - YN * CAP)))[..., None],
        (XN, ID_ROWS, LANES),
    ).astype(BF16)

    own = [features[:, h * LANES : (h + 1) * LANES] for h in range(2)]
    near = [[dom_shift(own[h], -o) for o in OFFSETS] for h in range(2)]
    arrived = []
    for h in range(2):
        feats = [near[h][0], near[h][1], own[h], near[h][2], near[h][3]]
        feats = [f.reshape(blocks_dev, BLOCK, LANES) for f in feats]
        sent = forward_products(src, slot, cnt, feats, vals, id_rows, h == 0)
        arrived.append(x_exchange(sent))
    ids = arrived[0][:, YN * CAP * BLOCK :, :][:, : YN * CAP].astype(F32)
    ids = ids.reshape(XN * YN * CAP, LANES)
    sums, far = [], []
    for h in range(2):
        blocks = gather_blocks(arrived[h], ids, blocks_dev)
        sums.append(blocks)
        for k in (1, 2, 3):
            to = lax.dynamic_index_in_dim(blocks, (me[0] + k) % YN, 0, keepdims=False)
            far.append(y_shift(to, k))
    activations, g0, g1, local_grad = dense(sums, far, me, weight, cotangent)

    parts = []
    for g in (g0, g1):
        grads = [g] + [y_shift(g, k) for k in (1, 2, 3)]
        back = x_exchange(reply_blocks(me, grads, ids, blocks_dev))
        terms = backward_products(src, slot, cnt, back, vals, blocks_dev)
        parts.append(terms[2])
        for term, o in zip((terms[0], terms[1], terms[3], terms[4]), OFFSETS):
            parts.append(dom_shift(term, o))
    feature_grad = final_sum(parts)

    rows = lax.axis_size("rows")
    channels = local_grad.shape[0]
    pieces = local_grad.reshape(rows, channels // rows, channels)
    piece = jnp.sum(
        lax.all_to_all(pieces, "rows", split_axis=0, concat_axis=0, tiled=True), axis=0
    )
    inner = 8
    outer = dom_count // inner
    near_groups = [[i * inner + j for j in range(inner)] for i in range(outer)]
    far_groups = [[i * inner + j for i in range(outer)] for j in range(inner)]
    piece = grouped_sum(piece, "dom", near_groups)
    piece = grouped_sum(piece, "dom", far_groups)
    whole = jnp.broadcast_to(piece[None], pieces.shape)
    weight_grad = lax.all_to_all(whole, "rows", split_axis=0, concat_axis=0, tiled=True)
    weight_grad = weight_grad.reshape(channels, channels)
    return (activations, feature_grad, weight_grad)


def solution(mesh):
    return jax.shard_map(
        per_device,
        mesh=mesh,
        in_specs=(
            P(("dom", "rows"), None),
            P(),
            P(("dom", "rows"), None, None, None, None),
            P(("dom", "rows"), None, None),
            P(("dom", "rows"), None, None),
            P(("dom", "rows"), None),
            P(("dom", "rows"), None),
            P(("dom", "rows"), None),
        ),
        out_specs=(P(("dom", "rows"), None), P(("dom", "rows"), None), P()),
        check_vma=False,
    )
```

```python
import functools

import jax
import jax.numpy as jnp
from jax import lax
from jax.experimental import pallas as pl
from jax.experimental.pallas import tpu as pltpu
from jax.sharding import PartitionSpec as P

BLOCK = 128
HALF = 2
CAP = 2
XN = 4
YN = 4
LANES = 128
ID_ROWS = 16

OFFSETS = (-2, -1, 1, 2)
VMEM = pl.BlockSpec(memory_space=pltpu.VMEM)
SMEM = pl.BlockSpec(memory_space=pltpu.SMEM)
BF16 = jnp.bfloat16
F32 = jnp.float32


def params():
    return pltpu.CompilerParams(vmem_limit_bytes=24 * 1024 * 1024)


def cost(flops, nbytes):
    return pl.CostEstimate(flops=flops, bytes_accessed=nbytes, transcendentals=0)


def dom_shift(value, steps):
    count = lax.axis_size("dom")
    return lax.ppermute(value, "dom", [(i, (i + steps) % count) for i in range(count)])


def y_shift(value, steps):
    pairs = [(x * YN + y, x * YN + (y + steps) % YN) for x in range(XN) for y in range(YN)]
    return lax.ppermute(value, "rows", pairs)


X_GROUPS = [[x * YN + y for x in range(XN)] for y in range(YN)]


def x_exchange(value):
    return lax.all_to_all(
        value, "rows", split_axis=0, concat_axis=0, tiled=True, axis_index_groups=X_GROUPS
    )


def x_shift(value, steps):
    pairs = [(x * YN + y, (x + steps) % XN * YN + y) for x in range(XN) for y in range(YN)]
    return lax.ppermute(value, "rows", pairs)


def forward_kernel(half, src, slot, cnt, fm2, fm1, f0, fp1, fp2, vals, ids, out, acc):
    acc[...] = jnp.zeros_like(acc)
    feats = (fm2, fm1, f0, fp1, fp2)
    tiles_step = vals.shape[0] // len(feats)
    for k, feat in enumerate(feats):
        for t in range(tiles_step):
            n = k * tiles_step + t

            @pl.when(t < cnt[0, k])
            def _():
                block = feat[src[k, t], :, half * LANES : (half + 1) * LANES]
                acc[slot[k, t]] += jnp.dot(vals[n], block, preferred_element_type=F32)

    per_x = acc.shape[0] // XN
    for s in range(acc.shape[0]):
        out[s // per_x, pl.ds((s % per_x) * BLOCK, BLOCK), :] = acc[s].astype(BF16)
    if half == 0:
        for x in range(XN):
            out[x, pl.ds(per_x * BLOCK, ID_ROWS), :] = ids[x]


def forward_products(src, slot, cnt, feats, vals, ids, half):
    slots = XN * YN * CAP
    rows = YN * CAP * BLOCK + (ID_ROWS if half == 0 else 0)
    return pl.pallas_call(
        functools.partial(forward_kernel, half),
        out_shape=jax.ShapeDtypeStruct((XN, rows, LANES), BF16),
        in_specs=[SMEM] * 3 + [VMEM] * 7,
        out_specs=VMEM,
        scratch_shapes=[pltpu.VMEM((slots, BLOCK, LANES), F32)],
        compiler_params=params(),
        cost_estimate=cost(vals.shape[0] * 2 * BLOCK * BLOCK * LANES, 9 << 20),
        name="tile_forward",
    )(src, slot, cnt, *feats, vals, ids)


def gather_kernel(blocks_dev, me, recv, ids, *refs):
    if len(refs) > 4:
        total = refs[0][...]
        for k in (1, 2, 3):
            total = total + refs[k][...].astype(F32)
        refs[4][...] = total.astype(BF16)
        refs = refs[5:]
    for k, out in enumerate(refs):
        y = lax.rem(me[0] + k, YN)
        for b in range(blocks_dev):
            total = jnp.zeros((BLOCK, LANES), F32)
            for x in range(XN):
                for c in range(CAP):
                    j = y * CAP + c
                    hit = ids[pl.ds(x * YN * CAP + j, 1), :] == float(b)
                    start = pl.multiple_of(j * BLOCK, BLOCK)
                    part = recv[x, pl.ds(start, BLOCK), :].astype(F32)
                    total = total + jnp.where(hit, part, 0.0)
            out[pl.ds(b * BLOCK, BLOCK), :] = total.astype(out.dtype)


def gather_blocks(me, recv, ids, blocks_dev, earlier=()):
    nodes = blocks_dev * BLOCK
    half = jax.ShapeDtypeStruct((nodes, LANES), BF16)
    own = jax.ShapeDtypeStruct((nodes, LANES), F32)
    outs = (own, half, half, half)
    if earlier:
        outs = (half,) + outs
    return pl.pallas_call(
        functools.partial(gather_kernel, blocks_dev),
        out_shape=outs,
        in_specs=[SMEM] + [VMEM] * (2 + len(earlier)),
        out_specs=(VMEM,) * len(outs),
        compiler_params=params(),
        cost_estimate=cost(1 << 20, 4 << 20),
        name="block_sums",
    )(me, recv, ids, *earlier)


def dense_kernel(me, agg0, own, far1, far2, far3, weight, cot, act, g0, g1, s1, s2, s3, mine, wg):
    total = own[...]
    for far in (far1, far2, far3):
        total = total + far[...].astype(F32)
    agg = jnp.concatenate([agg0[...], total.astype(BF16)], axis=1)
    w = weight[...]
    pre = jnp.dot(agg, w, preferred_element_type=F32)
    sig = 1.0 / (1.0 + jnp.exp(-pre))
    act[...] = (pre * sig).astype(BF16)
    slope = sig * (1.0 + pre * (1.0 - sig))
    pre_grad = (cot[...].astype(F32) * slope).astype(BF16)
    grad = lax.dot_general(
        pre_grad, w, (((1,), (1,)), ((), ())), preferred_element_type=F32
    ).astype(BF16)
    nodes = cot.shape[0]
    wg[...] = lax.dot_general(
        agg, pre_grad, (((0,), (0,)), ((), ())), preferred_element_type=F32
    )
    g0[...] = grad[:, :LANES]
    g1[...] = grad[:, LANES:]
    rows = wg.shape[0] // YN

    def piece(k):
        y = lax.rem(me[0] + k, YN)
        return wg[pl.ds(pl.multiple_of(y * rows, rows), rows), :]

    mine[...] = piece(0)
    for k, out in ((1, s1), (2, s2), (3, s3)):
        chunk = piece(k).astype(BF16)
        out[pl.ds(0, nodes), :] = grad[:, :LANES]
        out[pl.ds(nodes, rows), :] = chunk[:, :LANES]
        out[pl.ds(nodes + rows, rows), :] = chunk[:, LANES:]


def dense(me, agg0, own, far, weight, cot):
    nodes, channels = cot.shape
    rows = channels // YN
    half = jax.ShapeDtypeStruct((nodes, LANES), BF16)
    send = jax.ShapeDtypeStruct((nodes + 2 * rows, LANES), BF16)
    outs = (
        jax.ShapeDtypeStruct((nodes, channels), BF16),
        half,
        half,
        send,
        send,
        send,
        jax.ShapeDtypeStruct((rows, channels), F32),
    )
    return pl.pallas_call(
        dense_kernel,
        out_shape=outs,
        in_specs=[SMEM] + [VMEM] * 7,
        out_specs=(VMEM,) * len(outs),
        scratch_shapes=[pltpu.VMEM((channels, channels), F32)],
        compiler_params=params(),
        cost_estimate=cost(6 * nodes * channels * channels, 5 << 20),
        name="dense_layer",
    )(me, agg0, own, *far, weight, cot)


def pick_slots(blocks_dev, me, grads, ids, place):
    for k, grad in enumerate(grads):
        y = lax.rem(me[0] - k + YN, YN)
        blocks = [grad[pl.ds(b * BLOCK, BLOCK), :].astype(F32) for b in range(blocks_dev)]
        for c in range(CAP):
            j = y * CAP + c
            start = pl.multiple_of(j * BLOCK, BLOCK)
            for i in range(XN):
                x, out = place(i)
                row = ids[pl.ds(x * YN * CAP + j, 1), :]
                picked = jnp.where(row == 0.0, blocks[0], 0.0)
                for b in range(1, blocks_dev):
                    picked = jnp.where(row == float(b), blocks[b], picked)
                out[pl.ds(start, BLOCK), :] = picked.astype(BF16)


def reply0_kernel(blocks_dev, me, g0, r1, r2, r3, ids, mine, out):
    pick_slots(blocks_dev, me, (g0, r1, r2, r3), ids, lambda i: (i, out.at[i]))
    nodes = blocks_dev * BLOCK
    rows = mine.shape[0]
    left, right = mine[:, :LANES], mine[:, LANES:]
    for r in (r1, r2, r3):
        left = left + r[pl.ds(nodes, rows), :].astype(F32)
        right = right + r[pl.ds(nodes + rows, rows), :].astype(F32)
    base = YN * CAP * BLOCK
    per_x = rows // XN
    for x in range(XN):
        part = slice(x * per_x, (x + 1) * per_x)
        out[x, pl.ds(base, per_x), :] = left[part].astype(BF16)
        out[x, pl.ds(base + per_x, per_x), :] = right[part].astype(BF16)


def reply_first(me, grads, ids, mine, blocks_dev):
    rows = YN * CAP * BLOCK + 2 * (mine.shape[0] // XN)
    return pl.pallas_call(
        functools.partial(reply0_kernel, blocks_dev),
        out_shape=jax.ShapeDtypeStruct((XN, rows, LANES), BF16),
        in_specs=[SMEM] + [VMEM] * 6,
        out_specs=VMEM,
        compiler_params=params(),
        cost_estimate=cost(1 << 20, 4 << 20),
        name="slot_replies",
    )(me, *grads, ids, mine)


def reply1_kernel(blocks_dev, me, g0, r1, r2, r3, ids, *outs):
    pick_slots(
        blocks_dev, me, (g0, r1, r2, r3), ids, lambda i: (lax.rem(me[1] + i, XN), outs[i])
    )


def reply_second(me, grads, ids, blocks_dev):
    out = jax.ShapeDtypeStruct((YN * CAP * BLOCK, LANES), BF16)
    return pl.pallas_call(
        functools.partial(reply1_kernel, blocks_dev),
        out_shape=(out,) * XN,
        in_specs=[SMEM] + [VMEM] * 5,
        out_specs=(VMEM,) * XN,
        compiler_params=params(),
        cost_estimate=cost(1 << 20, 4 << 20),
        name="slot_replies",
    )(me, *grads, ids)


def tile_sums(src, slot, cnt, vals, acc, block_of, store):
    steps = cnt.shape[1]
    tiles_step = vals.shape[0] // steps
    for k in range(steps):
        acc[...] = jnp.zeros_like(acc)
        for t in range(tiles_step):
            n = k * tiles_step + t

            @pl.when(t < cnt[0, k])
            def _():
                acc[src[k, t]] += lax.dot_general(
                    vals[n],
                    block_of(slot[k, t]),
                    (((0,), (0,)), ((), ())),
                    preferred_element_type=F32,
                )

        store(k)


def backward0_kernel(src, slot, cnt, ret, vals, out, own, piece, acc):
    per_x = YN * CAP

    def block_of(s):
        start = pl.multiple_of(lax.rem(s, per_x) * BLOCK, BLOCK)
        return ret[lax.div(s, per_x), pl.ds(start, BLOCK), :]

    def store(k):
        for b in range(acc.shape[0]):
            if k == HALF:
                own[pl.ds(b * BLOCK, BLOCK), :] = acc[b]
            else:
                out[k, pl.ds(b * BLOCK, BLOCK), :] = acc[b].astype(BF16)

    tile_sums(src, slot, cnt, vals, acc, block_of, store)
    base = per_x * BLOCK
    rows = piece.shape[1]
    for side in range(2):
        total = ret[0, pl.ds(base + side * rows, rows), :].astype(F32)
        for x in range(1, XN):
            total = total + ret[x, pl.ds(base + side * rows, rows), :].astype(F32)
        for i in range(piece.shape[0]):
            piece[i, :, side * LANES : (side + 1) * LANES] = total


def backward_first(src, slot, cnt, ret, vals, blocks_dev, copies):
    nodes = blocks_dev * BLOCK
    rows = (ret.shape[1] - YN * CAP * BLOCK) // 2
    return pl.pallas_call(
        backward0_kernel,
        out_shape=(
            jax.ShapeDtypeStruct((2 * HALF + 1, nodes, LANES), BF16),
            jax.ShapeDtypeStruct((nodes, LANES), F32),
            jax.ShapeDtypeStruct((copies, rows, 2 * LANES), F32),
        ),
        in_specs=[SMEM] * 3 + [VMEM] * 2,
        out_specs=(VMEM,) * 3,
        scratch_shapes=[pltpu.VMEM((blocks_dev, BLOCK, LANES), F32)],
        compiler_params=params(),
        cost_estimate=cost(vals.shape[0] * 2 * BLOCK * BLOCK * LANES, 9 << 20),
        name="tile_backward",
    )(src, slot, cnt, ret, vals)


def backward1_kernel(
    src, slot, cnt, me, b0, b1, b2, b3, vals, first, om2, om1, op1, op2, own, acc, ret
):
    per_x = YN * CAP
    for k, back in enumerate((b0, b1, b2, b3)):
        ret[lax.rem(me[1] - k + XN, XN)] = back[...]
    outs = (om2, om1, own, op1, op2)

    def block_of(s):
        start = pl.multiple_of(lax.rem(s, per_x) * BLOCK, BLOCK)
        return ret[lax.div(s, per_x), pl.ds(start, BLOCK), :]

    def store(k):
        for b in range(acc.shape[0]):
            spot = pl.ds(b * BLOCK, BLOCK)
            if k == HALF:
                own[spot, :] = acc[b]
            else:
                outs[k][spot, :LANES] = first[k, spot, :]
                outs[k][spot, LANES:] = acc[b].astype(BF16)

    tile_sums(src, slot, cnt, vals, acc, block_of, store)


def backward_second(src, slot, cnt, me, back, vals, first, blocks_dev):
    nodes = blocks_dev * BLOCK
    send = jax.ShapeDtypeStruct((nodes, 2 * LANES), BF16)
    own = jax.ShapeDtypeStruct((nodes, LANES), F32)
    return pl.pallas_call(
        backward1_kernel,
        out_shape=(send,) * 4 + (own,),
        in_specs=[SMEM] * 4 + [VMEM] * 6,
        out_specs=(VMEM,) * 5,
        scratch_shapes=[
            pltpu.VMEM((blocks_dev, BLOCK, LANES), F32),
            pltpu.VMEM((XN, YN * CAP * BLOCK, LANES), BF16),
        ],
        compiler_params=params(),
        cost_estimate=cost(vals.shape[0] * 2 * BLOCK * BLOCK * LANES, 9 << 20),
        name="tile_backward",
    )(src, slot, cnt, me, *back, vals, first)


def final_kernel(own0, own1, r1, r2, r3, r4, out):
    for h, own in enumerate((own0, own1)):
        total = own[...]
        for r in (r1, r2, r3, r4):
            total = total + r[:, h * LANES : (h + 1) * LANES].astype(F32)
        out[:, h * LANES : (h + 1) * LANES] = total.astype(BF16)


def final_sum(*parts):
    return pl.pallas_call(
        final_kernel,
        out_shape=jax.ShapeDtypeStruct((parts[0].shape[0], 2 * LANES), BF16),
        in_specs=[VMEM] * len(parts),
        out_specs=VMEM,
        compiler_params=params(),
        cost_estimate=cost(1 << 20, 2 << 20),
        name="grad_sum",
    )(*parts)


def spread_kernel(parts, out):
    total = parts[0]
    for i in range(1, parts.shape[0]):
        total = total + parts[i]
    for i in range(out.shape[0]):
        out[i] = total


def sum_and_spread(parts, copies):
    return pl.pallas_call(
        spread_kernel,
        out_shape=jax.ShapeDtypeStruct((copies,) + parts.shape[1:], F32),
        in_specs=[VMEM],
        out_specs=VMEM,
        compiler_params=params(),
        cost_estimate=cost(1 << 16, 1 << 20),
        name="sum_and_spread",
    )(parts)


def dom_exchange(value, groups):
    return lax.all_to_all(
        value, "dom", split_axis=0, concat_axis=0, tiled=True, axis_index_groups=groups
    )


def per_device(
    features, weight, tile_values, tile_source, tile_slot, slot_block, tile_count, cotangent
):
    blocks_dev = features.shape[0] // BLOCK
    channels = features.shape[1]
    vals = tile_values.reshape(-1, BLOCK, BLOCK)
    src, slot, cnt = tile_source[0], tile_slot[0], tile_count
    rank = lax.axis_index("rows")
    me = jnp.stack([rank % YN, rank // YN]).astype(jnp.int32)
    id_rows = jnp.broadcast_to(
        jnp.pad(slot_block.reshape(XN, -1), ((0, 0), (0, ID_ROWS - YN * CAP)))[..., None],
        (XN, ID_ROWS, LANES),
    ).astype(BF16)
    inner = 8
    outer = lax.axis_size("dom") // inner
    near_groups = [[i * inner + j for j in range(inner)] for i in range(outer)]
    far_groups = [[i * inner + j for i in range(outer)] for j in range(inner)]

    near = [dom_shift(features, -o) for o in OFFSETS]
    feats = [near[0], near[1], features, near[2], near[3]]
    feats = [f.reshape(blocks_dev, BLOCK, channels) for f in feats]
    got0 = x_exchange(forward_products(src, slot, cnt, feats, vals, id_rows, 0))
    got1 = x_exchange(forward_products(src, slot, cnt, feats, vals, id_rows, 1))
    ids = got0[:, YN * CAP * BLOCK :, :][:, : YN * CAP].astype(F32)
    ids = ids.reshape(XN * YN * CAP, LANES)
    sums = gather_blocks(me, got0, ids, blocks_dev)
    far = [y_shift(sums[k], k) for k in (1, 2, 3)]
    agg0, *sums = gather_blocks(me, got1, ids, blocks_dev, (sums[0], *far))
    far = [y_shift(sums[k], k) for k in (1, 2, 3)]
    activations, g0, g1, s1, s2, s3, mine = dense(me, agg0, sums[0], far, weight, cotangent)

    grads = [g0] + [y_shift(s, k) for k, s in ((1, s1), (2, s2), (3, s3))]
    back0 = x_exchange(reply_first(me, grads, ids, mine, blocks_dev))
    grads = [g1] + [y_shift(g1, k) for k in (1, 2, 3)]
    reply = reply_second(me, grads, ids, blocks_dev)
    back1 = [reply[0]] + [x_shift(reply[k], k) for k in (1, 2, 3)]
    first, own0, piece = backward_first(src, slot, cnt, back0, vals, blocks_dev, inner)
    piece = sum_and_spread(dom_exchange(piece, near_groups), outer)
    *terms, own1 = backward_second(src, slot, cnt, me, back1, vals, first, blocks_dev)
    terms = [dom_shift(t, o) for t, o in zip(terms, OFFSETS)]
    piece = sum_and_spread(dom_exchange(piece, far_groups), XN * YN)
    whole = lax.all_to_all(piece, "rows", split_axis=0, concat_axis=0, tiled=True)
    whole = whole.reshape(XN, YN, channels // (XN * YN), channels)
    weight_grad = whole.transpose(1, 0, 2, 3).reshape(channels, channels)
    feature_grad = final_sum(own0, own1, *terms)
    return (activations, feature_grad, weight_grad)


def solution(mesh):
    return jax.shard_map(
        per_device,
        mesh=mesh,
        in_specs=(
            P(("dom", "rows"), None),
            P(),
            P(("dom", "rows"), None, None, None, None),
            P(("dom", "rows"), None, None),
            P(("dom", "rows"), None, None),
            P(("dom", "rows"), None),
            P(("dom", "rows"), None),
            P(("dom", "rows"), None),
        ),
        out_specs=(P(("dom", "rows"), None), P(("dom", "rows"), None), P()),
        check_vma=False,
    )
```

```python
import functools

import jax
import jax.numpy as jnp
from jax import lax
from jax.experimental import pallas as pl
from jax.experimental.pallas import tpu as pltpu
from jax.sharding import PartitionSpec as P

BLOCK = 128
HALF = 2
CAP = 2
XN = 4
YN = 4
LANES = 128
ID_ROWS = 16

OFFSETS = (-2, -1, 1, 2)
VMEM = pl.BlockSpec(memory_space=pltpu.VMEM)
ANY = pl.BlockSpec(memory_space=pl.ANY)
SMEM = pl.BlockSpec(memory_space=pltpu.SMEM)
GATHER_FLOPS = 10**11
REPLY_FLOPS = 10**11
BACK_FLOPS = 10**11
FINAL_FLOPS = 2*10**10
BF16 = jnp.bfloat16
F32 = jnp.float32


def params():
    return pltpu.CompilerParams(vmem_limit_bytes=24 * 1024 * 1024)


def cost(flops, nbytes):
    return pl.CostEstimate(flops=flops, bytes_accessed=nbytes, transcendentals=0)


def dom_shift(value, steps):
    count = lax.axis_size("dom")
    return lax.ppermute(value, "dom", [(i, (i + steps) % count) for i in range(count)])


Y_GROUPS = [[x * YN + y for y in range(YN)] for x in range(XN)]


def y_exchange(value):
    return lax.all_to_all(
        value, "rows", split_axis=0, concat_axis=0, tiled=True, axis_index_groups=Y_GROUPS
    )


def x_shift(value, steps):
    pairs = [(x * YN + y, (x + steps) % XN * YN + y) for x in range(XN) for y in range(YN)]
    return lax.ppermute(value, "rows", pairs)


def forward_kernel(src, slot, cnt, me, fm2, fm1, f0, fp1, fp2, vals, ids, *refs):
    outs, acc = refs[:-1], refs[-1]
    acc[...] = jnp.zeros_like(acc)
    feats = (fm2, fm1, f0, fp1, fp2)
    tiles_step = vals.shape[0] // len(feats)
    for k, feat in enumerate(feats):
        for t in range(tiles_step):
            live = t < cnt[0, k]
            block = feat[src[k, t]]
            block = jnp.where(live, block, jnp.zeros_like(block))
            acc[slot[k, t]] += jnp.dot(
                vals[k * tiles_step + t], block, preferred_element_type=F32
            )
    per_x = acc.shape[0] // XN
    for k in range(XN):
        x = lax.rem(me[1] + k, XN)
        for j in range(per_x):
            total = acc[x * per_x + j].astype(BF16)
            for h in range(2):
                part = total[:, h * LANES : (h + 1) * LANES]
                outs[h * XN + k][pl.ds(j * BLOCK, BLOCK), :] = part
        outs[k][pl.ds(per_x * BLOCK, ID_ROWS), :] = ids[x]


def forward_products(src, slot, cnt, me, feats, vals, ids):
    slots = XN * YN * CAP
    rows = YN * CAP * BLOCK
    first = jax.ShapeDtypeStruct((rows + ID_ROWS, LANES), BF16)
    second = jax.ShapeDtypeStruct((rows, LANES), BF16)
    return pl.pallas_call(
        forward_kernel,
        out_shape=(first,) * XN + (second,) * XN,
        in_specs=[SMEM] * 4 + [VMEM] * 7,
        out_specs=(VMEM,) * (2 * XN),
        scratch_shapes=[pltpu.VMEM((slots, BLOCK, 2 * LANES), F32)],
        compiler_params=params(),
        cost_estimate=cost(vals.shape[0] * 4 * BLOCK * BLOCK * LANES, 9 << 20),
        name="tile_forward",
    )(src, slot, cnt, me, *feats, vals, ids)


def id_row(ids, j):
    return ids[j : j + 1, :]


def gather_kernel(blocks_dev, n_after, *refs):
    recv, with_ids = refs[0:XN], refs[XN : 2 * XN]
    out = refs[2 * XN + n_after]
    base = YN * CAP * BLOCK
    ids = [w[pl.ds(base, ID_ROWS), :].astype(F32) for w in with_ids]
    for y in range(YN):
        totals = [jnp.zeros((BLOCK, LANES), F32) for _ in range(blocks_dev)]
        for k in range(XN):
            for c in range(CAP):
                j = y * CAP + c
                row = id_row(ids[k], j)
                part = recv[k][pl.ds(j * BLOCK, BLOCK), :].astype(F32)
                for b in range(blocks_dev):
                    totals[b] = totals[b] + jnp.where(row == float(b), part, 0.0)
        for b in range(blocks_dev):
            out[y, pl.ds(b * BLOCK, BLOCK), :] = totals[b].astype(BF16)


def gather_blocks(recv, with_ids, blocks_dev, after=()):
    return pl.pallas_call(
        functools.partial(gather_kernel, blocks_dev, len(after)),
        out_shape=jax.ShapeDtypeStruct((YN, blocks_dev * BLOCK, LANES), BF16),
        in_specs=[VMEM] * (2 * XN) + [ANY] * len(after),
        out_specs=VMEM,
        compiler_params=params(),
        cost_estimate=cost(GATHER_FLOPS, 4 << 20),
        name="block_sums",
    )(*recv, *with_ids, *after)


def dense_kernel(p0, p1, weight, cot, act, s0, s1, wg):
    halves = []
    for p in (p0, p1):
        total = p[0].astype(F32)
        for y in range(1, YN):
            total = total + p[y].astype(F32)
        halves.append(total.astype(BF16))
    agg = jnp.concatenate(halves, axis=1)
    w = weight[...]
    pre = jnp.dot(agg, w, preferred_element_type=F32)
    sig = 1.0 / (1.0 + jnp.exp(-pre))
    act[...] = (pre * sig).astype(BF16)
    slope = sig * (1.0 + pre * (1.0 - sig))
    pre_grad = (cot[...].astype(F32) * slope).astype(BF16)
    grad = lax.dot_general(
        pre_grad, w, (((1,), (1,)), ((), ())), preferred_element_type=F32
    ).astype(BF16)
    nodes = cot.shape[0]
    wg[...] = lax.dot_general(
        agg, pre_grad, (((0,), (0,)), ((), ())), preferred_element_type=F32
    )
    rows = wg.shape[0] // YN
    for y in range(YN):
        chunk = wg[pl.ds(y * rows, rows), :].astype(BF16)
        s0[y, pl.ds(0, nodes), :] = grad[:, :LANES]
        s0[y, pl.ds(nodes, rows), :] = chunk[:, :LANES]
        s0[y, pl.ds(nodes + rows, rows), :] = chunk[:, LANES:]
        s1[y] = grad[:, LANES:]


def dense(p0, p1, weight, cot):
    nodes, channels = cot.shape
    rows = channels // YN
    outs = (
        jax.ShapeDtypeStruct((nodes, channels), BF16),
        jax.ShapeDtypeStruct((YN, nodes + 2 * rows, LANES), BF16),
        jax.ShapeDtypeStruct((YN, nodes, LANES), BF16),
    )
    return pl.pallas_call(
        dense_kernel,
        out_shape=outs,
        in_specs=[VMEM] * 4,
        out_specs=(VMEM,) * len(outs),
        scratch_shapes=[pltpu.VMEM((channels, channels), F32)],
        compiler_params=params(),
        cost_estimate=cost(6 * nodes * channels * channels, 5 << 20),
        name="dense_layer",
    )(p0, p1, weight, cot)


def reply_kernel(blocks_dev, carries, n_after, *refs):
    me, grads, with_ids = refs[0], refs[1], refs[2 : 2 + XN]
    outs = refs[2 + XN + n_after :]
    nodes = blocks_dev * BLOCK
    base = YN * CAP * BLOCK
    ids = [w[pl.ds(base, ID_ROWS), :].astype(F32) for w in with_ids]
    for y in range(YN):
        blocks = [grads[y, pl.ds(b * BLOCK, BLOCK), :].astype(F32) for b in range(blocks_dev)]
        for c in range(CAP):
            j = y * CAP + c
            for k in range(XN):
                row = id_row(ids[k], j)
                picked = jnp.where(row == 0.0, blocks[0], 0.0)
                for b in range(1, blocks_dev):
                    picked = jnp.where(row == float(b), blocks[b], picked)
                outs[k][pl.ds(j * BLOCK, BLOCK), :] = picked.astype(BF16)
    if carries:
        total = refs[-1]
        outs = outs[:-1]
        rows = total.shape[0] // 2
        total[...] = grads[0, pl.ds(nodes, 2 * rows), :].astype(F32)
        for y in range(1, YN):
            total[...] += grads[y, pl.ds(nodes, 2 * rows), :].astype(F32)
        per_x = rows // XN
        for k in range(XN):
            start = pl.multiple_of(lax.rem(me[1] - k + XN, XN) * per_x, per_x)
            for side in range(2):
                part = total[pl.ds(side * rows + start, per_x), :].astype(BF16)
                outs[k][pl.ds(base + side * per_x, per_x), :] = part


def reply_slots(me, grads, with_ids, blocks_dev, carries, after=()):
    rows = YN * CAP * BLOCK
    extra = grads.shape[1] - blocks_dev * BLOCK
    out = jax.ShapeDtypeStruct((rows + extra // XN, LANES), BF16)
    return pl.pallas_call(
        functools.partial(reply_kernel, blocks_dev, carries, len(after)),
        out_shape=(out,) * XN,
        in_specs=[SMEM] + [VMEM] * (1 + XN) + [ANY] * len(after),
        out_specs=(VMEM,) * XN,
        scratch_shapes=[pltpu.VMEM((extra, LANES), F32)] if carries else [],
        compiler_params=params(),
        cost_estimate=cost(REPLY_FLOPS, 4 << 20),
        name="slot_replies",
    )(me, grads, *with_ids, *after)


def piece_kernel(b0, b1, b2, b3, after, out):
    base = YN * CAP * BLOCK
    rows = out.shape[1]
    for side in range(2):
        spot = pl.ds(base + side * rows, rows)
        total = b0[spot, :].astype(F32)
        for arrived in (b1, b2, b3):
            total = total + arrived[spot, :].astype(F32)
        for i in range(out.shape[0]):
            out[i, :, side * LANES : (side + 1) * LANES] = total


def piece_sum(back, copies, after):
    rows = (back[0].shape[0] - YN * CAP * BLOCK) // 2
    return pl.pallas_call(
        piece_kernel,
        out_shape=jax.ShapeDtypeStruct((copies, rows, 2 * LANES), F32),
        in_specs=[VMEM] * XN + [ANY],
        out_specs=VMEM,
        compiler_params=params(),
        cost_estimate=cost(1 << 16, 1 << 20),
        name="piece_sum",
    )(*back, after)


def backward_kernel(src, slot, cnt, me, *refs):
    back, vals, outs, (acc, ret) = refs[: 2 * XN], refs[2 * XN], refs[2 * XN + 1 : -2], refs[-2:]
    per_x = YN * CAP
    for k in range(XN):
        x = lax.rem(me[1] + k, XN)
        for h in range(2):
            for j in range(per_x):
                part = back[h * XN + k][pl.ds(j * BLOCK, BLOCK), :]
                ret[x * per_x + j, :, h * LANES : (h + 1) * LANES] = part
    steps = cnt.shape[1]
    tiles_step = vals.shape[0] // steps
    acc[...] = jnp.zeros_like(acc)
    for k in range(steps):
        for t in range(tiles_step):
            block = ret[slot[k, t]]
            block = jnp.where(t < cnt[0, k], block, jnp.zeros_like(block))
            acc[k, src[k, t]] += lax.dot_general(
                vals[k * tiles_step + t],
                block,
                (((0,), (0,)), ((), ())),
                preferred_element_type=F32,
            )
    for k, out in enumerate(outs):
        for b in range(acc.shape[1]):
            out[pl.ds(b * BLOCK, BLOCK), :] = acc[k, b].astype(out.dtype)


def backward_products(src, slot, cnt, me, back0, back1, vals, blocks_dev):
    nodes = blocks_dev * BLOCK
    steps = cnt.shape[1]
    send = jax.ShapeDtypeStruct((nodes, 2 * LANES), BF16)
    own = jax.ShapeDtypeStruct((nodes, 2 * LANES), F32)
    return pl.pallas_call(
        backward_kernel,
        out_shape=(send, send, own, send, send),
        in_specs=[SMEM] * 4 + [VMEM] * (2 * XN + 1),
        out_specs=(VMEM,) * 5,
        scratch_shapes=[
            pltpu.VMEM((steps, blocks_dev, BLOCK, 2 * LANES), F32),
            pltpu.VMEM((XN * YN * CAP, BLOCK, 2 * LANES), BF16),
        ],
        compiler_params=params(),
        cost_estimate=cost(BACK_FLOPS, 9 << 20),
        name="tile_backward",
    )(src, slot, cnt, me, *back0, *back1, vals)


def final_kernel(own, r1, r2, r3, r4, out):
    total = own[...]
    for r in (r1, r2, r3, r4):
        total = total + r[...].astype(F32)
    out[...] = total.astype(BF16)


def final_sum(*parts):
    return pl.pallas_call(
        final_kernel,
        out_shape=jax.ShapeDtypeStruct(parts[0].shape, BF16),
        in_specs=[VMEM] * len(parts),
        out_specs=VMEM,
        compiler_params=params(),
        cost_estimate=cost(FINAL_FLOPS, 2 << 20),
        name="grad_sum",
    )(*parts)


def spread_kernel(parts, out):
    total = parts[0]
    for i in range(1, parts.shape[0]):
        total = total + parts[i]
    for i in range(out.shape[0]):
        out[i] = total


def sum_and_spread(parts, copies):
    return pl.pallas_call(
        spread_kernel,
        out_shape=jax.ShapeDtypeStruct((copies,) + parts.shape[1:], F32),
        in_specs=[VMEM],
        out_specs=VMEM,
        compiler_params=params(),
        cost_estimate=cost(1 << 16, 1 << 20),
        name="sum_and_spread",
    )(parts)


def dom_exchange(value, groups):
    return lax.all_to_all(
        value, "dom", split_axis=0, concat_axis=0, tiled=True, axis_index_groups=groups
    )


def per_device(
    features, weight, tile_values, tile_source, tile_slot, slot_block, tile_count, cotangent
):
    blocks_dev = features.shape[0] // BLOCK
    channels = features.shape[1]
    vals = tile_values.reshape(-1, BLOCK, BLOCK)
    src, slot, cnt = tile_source[0], tile_slot[0], tile_count
    rank = lax.axis_index("rows")
    me = jnp.stack([rank % YN, rank // YN]).astype(jnp.int32)
    id_rows = jnp.broadcast_to(
        jnp.pad(slot_block.reshape(XN, -1), ((0, 0), (0, ID_ROWS - YN * CAP)))[..., None],
        (XN, ID_ROWS, LANES),
    ).astype(BF16)
    inner = 8
    outer = lax.axis_size("dom") // inner
    near_groups = [[i * inner + j for j in range(inner)] for i in range(outer)]
    far_groups = [[i * inner + j for i in range(outer)] for j in range(inner)]

    near = [dom_shift(features, -o) for o in OFFSETS]
    feats = [near[0], near[1], features, near[2], near[3]]
    feats = [f.reshape(blocks_dev, BLOCK, channels) for f in feats]
    sent = forward_products(src, slot, cnt, me, feats, vals, id_rows)
    got0 = [sent[0]] + [x_shift(sent[k], k) for k in range(1, XN)]
    got1 = [sent[XN]] + [x_shift(sent[XN + k], k) for k in range(1, XN)]
    sums0 = gather_blocks(got0, got0, blocks_dev)
    p0 = y_exchange(sums0)
    p1 = y_exchange(gather_blocks(got1, got0, blocks_dev, (sums0,)))
    activations, s0, s1 = dense(p0, p1, weight, cotangent)

    reply0 = reply_slots(me, y_exchange(s0), got0, blocks_dev, True)
    back0 = [reply0[0]] + [x_shift(reply0[k], -k) for k in range(1, XN)]
    reply1 = reply_slots(me, y_exchange(s1), got0, blocks_dev, False, (reply0[0],))
    back1 = [reply1[0]] + [x_shift(reply1[k], -k) for k in range(1, XN)]
    piece = piece_sum(back0, inner, reply1[0])
    terms = list(backward_products(src, slot, cnt, me, back0, back1, vals, blocks_dev))
    own = terms.pop(HALF)
    terms = [dom_shift(t, o) for t, o in zip(terms, OFFSETS)]
    piece = sum_and_spread(dom_exchange(piece, near_groups), outer)
    piece = sum_and_spread(dom_exchange(piece, far_groups), XN * YN)
    whole = lax.all_to_all(piece, "rows", split_axis=0, concat_axis=0, tiled=True)
    whole = whole.reshape(XN, YN, channels // (XN * YN), channels)
    weight_grad = whole.transpose(1, 0, 2, 3).reshape(channels, channels)
    feature_grad = final_sum(own, *terms)
    return (activations, feature_grad, weight_grad)


def solution(mesh):
    return jax.shard_map(
        per_device,
        mesh=mesh,
        in_specs=(
            P(("dom", "rows"), None),
            P(),
            P(("dom", "rows"), None, None, None, None),
            P(("dom", "rows"), None, None),
            P(("dom", "rows"), None, None),
            P(("dom", "rows"), None),
            P(("dom", "rows"), None),
            P(("dom", "rows"), None),
        ),
        out_specs=(P(("dom", "rows"), None), P(("dom", "rows"), None), P()),
        check_vma=False,
    )
```

```python
import functools

import jax
import jax.numpy as jnp
from jax import lax
from jax.experimental import pallas as pl
from jax.experimental.pallas import tpu as pltpu
from jax.sharding import PartitionSpec as P

BLOCK = 128
HALF = 2
CAP = 2
XN = 4
YN = 4
INNER = 8
LANES = 128
ID_ROWS = 16

OFFSETS = (-2, -1, 1, 2)
VMEM = pl.BlockSpec(memory_space=pltpu.VMEM)
SMEM = pl.BlockSpec(memory_space=pltpu.SMEM)
BF16 = jnp.bfloat16
F32 = jnp.float32

GATHER_FLOPS = 1 << 20
DENSE_FLOPS = 1 << 28
REPLY_FLOPS = 10**10
BACK_FLOPS = 10**10
FINAL_FLOPS = 10**10
SPREAD_FLOPS = 1 << 16


def kernel_call(body, name, outs, ins, mib, flops, scratch=()):
    nbytes = sum(a.size * a.dtype.itemsize for _, a in ins)
    return pl.pallas_call(
        body,
        out_shape=outs,
        in_specs=[space for space, _ in ins],
        out_specs=jax.tree.map(lambda _: VMEM, outs),
        scratch_shapes=list(scratch),
        compiler_params=pltpu.CompilerParams(vmem_limit_bytes=mib << 20),
        cost_estimate=pl.CostEstimate(flops=flops, bytes_accessed=nbytes, transcendentals=0),
        name=name,
    )(*[a for _, a in ins])


def dom_shift(value, steps):
    count = lax.axis_size("dom")
    return lax.ppermute(value, "dom", [(i, (i + steps) % count) for i in range(count)])


def y_shift(value, steps):
    pairs = [(x * YN + y, x * YN + (y + steps) % YN) for x in range(XN) for y in range(YN)]
    return lax.ppermute(value, "rows", pairs)


def x_shift(value, steps):
    pairs = [(x * YN + y, (x + steps) % XN * YN + y) for x in range(XN) for y in range(YN)]
    return lax.ppermute(value, "rows", pairs)


X_GROUPS = [[x * YN + y for x in range(XN)] for y in range(YN)]
Y_GROUPS = [[x * YN + y for y in range(YN)] for x in range(XN)]


def exchange(value, axis, groups=None):
    return lax.all_to_all(
        value, axis, split_axis=0, concat_axis=0, tiled=True, axis_index_groups=groups
    )


def forward_kernel(src, slot, cnt, fm2, fm1, f0, fp1, fp2, vals, ids, out, acc):
    acc[...] = jnp.zeros_like(acc)
    feats = (fm2, fm1, f0, fp1, fp2)
    tiles_step = vals.shape[0] // len(feats)
    for k, feat in enumerate(feats):
        for t in range(tiles_step):
            block = feat[src[k, t]]
            block = jnp.where(t < cnt[0, k], block, jnp.zeros_like(block))
            acc[slot[k, t]] += jnp.dot(
                vals[k * tiles_step + t], block, preferred_element_type=F32
            )
    per_x = YN * CAP
    for x in range(XN):
        for j in range(per_x):
            out[x, pl.ds(j * BLOCK, BLOCK), :] = acc[x * per_x + j].astype(BF16)
        out[x, pl.ds(per_x * BLOCK, ID_ROWS), :] = ids[x]


def forward_products(src, slot, cnt, feats, vals, ids):
    channels = feats[0].shape[2]
    rows = YN * CAP * BLOCK + ID_ROWS
    ins = [(SMEM, src), (SMEM, slot), (SMEM, cnt)]
    ins += [(VMEM, a) for a in (*feats, vals, ids)]
    return kernel_call(
        forward_kernel,
        "tile_forward",
        jax.ShapeDtypeStruct((XN, rows, channels), BF16),
        ins,
        12,
        vals.size * 2 * channels,
        [pltpu.VMEM((XN * YN * CAP, BLOCK, channels), F32)],
    )


def gather_kernel(blocks_dev, recv, out, ids_out):
    base = YN * CAP * BLOCK
    for x in range(XN):
        ids = recv[x, pl.ds(base, ID_ROWS), :].astype(F32)
        ids_out[pl.ds(x * YN * CAP, YN * CAP), :] = ids[: YN * CAP]
    chunk = 32
    for y in range(YN):
        for start in range(0, BLOCK, chunk):
            totals = [jnp.zeros((chunk, out.shape[2]), F32) for _ in range(blocks_dev)]
            for x in range(XN):
                for c in range(CAP):
                    j = y * CAP + c
                    n = x * YN * CAP + j
                    row = ids_out[n : n + 1, :]
                    part = recv[x, pl.ds(j * BLOCK + start, chunk), :].astype(F32)
                    for b in range(blocks_dev):
                        totals[b] = totals[b] + jnp.where(row == float(b), part, 0.0)
            for b in range(blocks_dev):
                out[y, pl.ds(b * BLOCK + start, chunk), :] = totals[b].astype(BF16)


def gather_blocks(recv, blocks_dev):
    channels = recv.shape[2]
    return kernel_call(
        functools.partial(gather_kernel, blocks_dev),
        "block_sums",
        (
            jax.ShapeDtypeStruct((YN, blocks_dev * BLOCK, channels), BF16),
            jax.ShapeDtypeStruct((XN * YN * CAP, channels), F32),
        ),
        [(VMEM, recv)],
        6,
        GATHER_FLOPS,
    )


def dense_kernel(parts, weight, cot, act, grad, wgrad):
    total = parts[0].astype(F32)
    for y in range(1, YN):
        total = total + parts[y].astype(F32)
    agg = total.astype(BF16)
    w = weight[...]
    pre = jnp.dot(agg, w, preferred_element_type=F32)
    sig = 1.0 / (1.0 + jnp.exp(-pre))
    act[...] = (pre * sig).astype(BF16)
    slope = sig * (1.0 + pre * (1.0 - sig))
    pre_grad = (cot[...].astype(F32) * slope).astype(BF16)
    grad[...] = lax.dot_general(
        pre_grad, w, (((1,), (1,)), ((), ())), preferred_element_type=F32
    ).astype(BF16)
    wgrad[...] = lax.dot_general(
        agg, pre_grad, (((0,), (0,)), ((), ())), preferred_element_type=F32
    )


def dense(parts, weight, cot):
    nodes, channels = cot.shape
    full = jax.ShapeDtypeStruct((nodes, channels), BF16)
    return kernel_call(
        dense_kernel,
        "dense_layer",
        (full, full, jax.ShapeDtypeStruct((channels, channels), F32)),
        [(VMEM, parts), (VMEM, weight), (VMEM, cot)],
        10,
        DENSE_FLOPS,
    )


def reply_kernel(blocks_dev, me, g0, r1, r2, r3, ids, *outs):
    chunk = 32
    for k, grads in enumerate((g0, r1, r2, r3)):
        y = lax.rem(me[0] - k + YN, YN)
        rows = {}
        for i in range(XN):
            x = lax.rem(me[1] - i + XN, XN)
            for c in range(CAP):
                rows[i, c] = ids[pl.ds(x * YN * CAP + y * CAP + c, 1), :]
        for start in range(0, BLOCK, chunk):
            blocks = [
                grads[pl.ds(b * BLOCK + start, chunk), :].astype(F32) for b in range(blocks_dev)
            ]
            for (i, c), row in rows.items():
                picked = jnp.where(row == 0.0, blocks[0], 0.0)
                for b in range(1, blocks_dev):
                    picked = jnp.where(row == float(b), blocks[b], picked)
                spot = pl.multiple_of((y * CAP + c) * BLOCK + start, chunk)
                outs[i][pl.ds(spot, chunk), :] = picked.astype(BF16)


def reply_slots(me, grads, ids, blocks_dev):
    out = jax.ShapeDtypeStruct((YN * CAP * BLOCK, ids.shape[1]), BF16)
    return kernel_call(
        functools.partial(reply_kernel, blocks_dev),
        "slot_replies",
        (out,) * XN,
        [(SMEM, me)] + [(VMEM, a) for a in (*grads, ids)],
        6,
        REPLY_FLOPS,
    )


def backward_kernel(src, slot, cnt, me, b0, b1, b2, b3, vals, om2, om1, own, op1, op2, acc, ret):
    per_x = YN * CAP
    for k, back in enumerate((b0, b1, b2, b3)):
        x = lax.rem(me[1] + k, XN)
        for j in range(per_x):
            ret[x * per_x + j] = back[pl.ds(j * BLOCK, BLOCK), :]
    steps = cnt.shape[1]
    tiles_step = vals.shape[0] // steps
    acc[...] = jnp.zeros_like(acc)
    for k in range(steps):
        for t in range(tiles_step):
            block = ret[slot[k, t]]
            block = jnp.where(t < cnt[0, k], block, jnp.zeros_like(block))
            acc[k, src[k, t]] += lax.dot_general(
                vals[k * tiles_step + t],
                block,
                (((0,), (0,)), ((), ())),
                preferred_element_type=F32,
            )
    for k, out in enumerate((om2, om1, own, op1, op2)):
        for b in range(acc.shape[1]):
            out[pl.ds(b * BLOCK, BLOCK), :] = acc[k, b].astype(out.dtype)


def backward_products(src, slot, cnt, me, back, vals, blocks_dev):
    nodes, channels = blocks_dev * BLOCK, back[0].shape[1]
    steps = cnt.shape[1]
    send = jax.ShapeDtypeStruct((nodes, channels), BF16)
    own = jax.ShapeDtypeStruct((nodes, channels), F32)
    return kernel_call(
        backward_kernel,
        "tile_backward",
        (send, send, own, send, send),
        [(SMEM, a) for a in (src, slot, cnt, me)] + [(VMEM, a) for a in (*back, vals)],
        12,
        BACK_FLOPS,
        [
            pltpu.VMEM((steps, blocks_dev, BLOCK, channels), F32),
            pltpu.VMEM((XN * YN * CAP, BLOCK, channels), BF16),
        ],
    )


def final_kernel(own, r1, r2, r3, r4, out):
    total = own[...]
    for r in (r1, r2, r3, r4):
        total = total + r[...].astype(F32)
    out[...] = total.astype(BF16)


def final_sum(parts):
    return kernel_call(
        final_kernel,
        "grad_sum",
        jax.ShapeDtypeStruct(parts[0].shape, BF16),
        [(VMEM, a) for a in parts],
        4,
        FINAL_FLOPS,
    )


def spread_kernel(parts, out):
    total = parts[0]
    for i in range(1, parts.shape[0]):
        total = total + parts[i]
    for i in range(out.shape[0]):
        out[i] = total


def sum_and_spread(parts, copies):
    return kernel_call(
        spread_kernel,
        "sum_and_spread",
        jax.ShapeDtypeStruct((copies,) + parts.shape[1:], F32),
        [(VMEM, parts)],
        2,
        SPREAD_FLOPS,
    )


def summed_weight_grad(local_grad):
    channels = local_grad.shape[1]
    rows, dom = lax.axis_size("rows"), lax.axis_size("dom")
    outer = dom // INNER
    near = [[i * INNER + j for j in range(INNER)] for i in range(outer)]
    far = [[i * INNER + j for i in range(outer)] for j in range(INNER)]
    pieces = local_grad.reshape(rows, local_grad.shape[0] // rows, channels)
    piece = sum_and_spread(exchange(pieces, "rows"), INNER)
    piece = sum_and_spread(exchange(piece, "dom", near), outer)
    piece = sum_and_spread(exchange(piece, "dom", far), rows)
    return exchange(piece, "rows").reshape(local_grad.shape)


def per_device(
    features, weight, tile_values, tile_source, tile_slot, slot_block, tile_count, cotangent
):
    blocks_dev = features.shape[0] // BLOCK
    channels = features.shape[1]
    vals = tile_values.reshape(-1, BLOCK, BLOCK)
    src, slot, cnt = tile_source[0], tile_slot[0], tile_count
    rank = lax.axis_index("rows")
    me = jnp.stack([rank % YN, rank // YN]).astype(jnp.int32)
    id_rows = jnp.broadcast_to(
        jnp.pad(slot_block.reshape(XN, -1), ((0, 0), (0, ID_ROWS - YN * CAP)))[..., None],
        (XN, ID_ROWS, channels),
    ).astype(BF16)

    near = [dom_shift(features, -o) for o in OFFSETS]
    feats = [near[0], near[1], features, near[2], near[3]]
    feats = [f.reshape(blocks_dev, BLOCK, channels) for f in feats]
    sent = forward_products(src, slot, cnt, feats, vals, id_rows)
    sums, ids = gather_blocks(exchange(sent, "rows", X_GROUPS), blocks_dev)
    parts = exchange(sums, "rows", Y_GROUPS)
    activations, grad, local_grad = dense(parts, weight, cotangent)

    grads = [grad] + [y_shift(grad, k) for k in range(1, YN)]
    reply = reply_slots(me, grads, ids, blocks_dev)
    back = [reply[0]] + [x_shift(reply[k], -k) for k in range(1, XN)]
    terms = list(backward_products(src, slot, cnt, me, back, vals, blocks_dev))
    own = terms.pop(HALF)
    terms = [dom_shift(t, o) for t, o in zip(terms, OFFSETS)]
    weight_grad = summed_weight_grad(local_grad)
    feature_grad = final_sum([own, *terms])
    return (activations, feature_grad, weight_grad)


def solution(mesh):
    return jax.shard_map(
        per_device,
        mesh=mesh,
        in_specs=(
            P(("dom", "rows"), None),
            P(),
            P(("dom", "rows"), None, None, None, None),
            P(("dom", "rows"), None, None),
            P(("dom", "rows"), None, None),
            P(("dom", "rows"), None),
            P(("dom", "rows"), None),
            P(("dom", "rows"), None),
        ),
        out_specs=(P(("dom", "rows"), None), P(("dom", "rows"), None), P()),
        check_vma=False,
    )
```

```python
import functools

import jax
import jax.numpy as jnp
from jax import lax
from jax.experimental import pallas as pl
from jax.experimental.pallas import tpu as pltpu
from jax.sharding import PartitionSpec as P

BLOCK = 128
HALF = 2
CAP = 2
XN = 4
YN = 4
INNER = 8
LANES = 128
ID_ROWS = 8

OFFSETS = (-2, -1, 1, 2)
VMEM = pl.BlockSpec(memory_space=pltpu.VMEM)
HBM = pl.BlockSpec(memory_space=pltpu.HBM)
SMEM = pl.BlockSpec(memory_space=pltpu.SMEM)
BF16 = jnp.bfloat16
F32 = jnp.float32

GATHER_FLOPS = 1 << 20
DENSE_FLOPS = 1 << 28
REPLY_FLOPS = 2*10**9
BACK_FLOPS = 2*10**9
FINAL_FLOPS = 2*10**9
SPREAD_FLOPS = 1 << 16


def kernel_call(body, name, outs, ins, mib, flops, scratch=(), out_specs=None):
    nbytes = sum(a.size * a.dtype.itemsize for _, a in ins)
    return pl.pallas_call(
        body,
        out_shape=outs,
        in_specs=[space for space, _ in ins],
        out_specs=out_specs or jax.tree.map(lambda _: VMEM, outs),
        scratch_shapes=list(scratch),
        compiler_params=pltpu.CompilerParams(vmem_limit_bytes=mib << 20),
        cost_estimate=pl.CostEstimate(flops=flops, bytes_accessed=nbytes, transcendentals=0),
        name=name,
    )(*[a for _, a in ins])


def dom_shift(value, steps):
    count = lax.axis_size("dom")
    return lax.ppermute(value, "dom", [(i, (i + steps) % count) for i in range(count)])


def y_shift(value, steps):
    pairs = [(x * YN + y, x * YN + (y + steps) % YN) for x in range(XN) for y in range(YN)]
    return lax.ppermute(value, "rows", pairs)


def x_shift(value, steps):
    pairs = [(x * YN + y, (x + steps) % XN * YN + y) for x in range(XN) for y in range(YN)]
    return lax.ppermute(value, "rows", pairs)


X_GROUPS = [[x * YN + y for x in range(XN)] for y in range(YN)]
Y_GROUPS = [[x * YN + y for y in range(YN)] for x in range(XN)]


def exchange(value, axis, groups=None):
    return lax.all_to_all(
        value, axis, split_axis=0, concat_axis=0, tiled=True, axis_index_groups=groups
    )


def position():
    rank = lax.axis_index("rows")
    return lax.div(rank, YN), lax.rem(rank, YN)


def forward_kernel(src, slot, cnt, fm2, fm1, f0, fp1, fp2, vals, out, acc):
    acc[...] = jnp.zeros_like(acc)
    feats = (fm2, fm1, f0, fp1, fp2)
    tiles_step = vals.shape[0] // len(feats)
    for k, feat in enumerate(feats):
        for t in range(tiles_step):
            block = feat[src[t, k]]
            block = jnp.where(t < cnt[0, k], block, jnp.zeros_like(block))
            acc[slot[t, k]] += jnp.dot(
                vals[k * tiles_step + t], block, preferred_element_type=F32
            )
    for n in range(acc.shape[0]):
        out[n // CAP, pl.ds(n % CAP * BLOCK, BLOCK), :] = acc[n].astype(BF16)


def forward_products(src, slot, cnt, feats, vals):
    channels = feats[0].shape[2]
    return kernel_call(
        forward_kernel,
        "tile_forward",
        jax.ShapeDtypeStruct((XN * YN, CAP * BLOCK, channels), BF16),
        [(SMEM, a) for a in (src, slot, cnt)] + [(VMEM, a) for a in (*feats, vals)],
        12,
        vals.size * 2 * channels,
        [pltpu.VMEM((XN * YN * CAP, BLOCK, channels), F32)],
    )


def ids_kernel(own, i1, i2, i3, out):
    me_x, _ = position()
    out[...] = jnp.zeros_like(out)
    for k, ids in enumerate((own, i1, i2, i3)):
        out[pl.ds(lax.rem(me_x - k + XN, XN), 1), :] = ids[pl.ds(0, 1), :]


def column_ids(ids):
    return kernel_call(
        ids_kernel,
        "column_ids",
        jax.ShapeDtypeStruct(ids[0].shape, jnp.int32),
        [(VMEM, a) for a in ids],
        2,
        1 << 10,
    )


def dense_kernel(i0, i1, i2, i3, recv, weight, cot, act, grad, wgrad, acc):
    me_x, me_y = position()
    first = (me_x * YN + me_y) * CAP
    acc[...] = jnp.zeros_like(acc)
    for k, ids in enumerate((i0, i1, i2, i3)):
        y = lax.rem(me_y - k + YN, YN)
        for x in range(XN):
            for c in range(CAP):
                part = recv[x * YN + y, pl.ds(c * BLOCK, BLOCK), :]
                acc[ids[x, first + c]] += part.astype(F32)
    agg = acc[...].reshape(cot.shape).astype(BF16)
    w = weight[...]
    pre = jnp.dot(agg, w, preferred_element_type=F32)
    sig = 1.0 / (1.0 + jnp.exp(-pre))
    act[...] = (pre * sig).astype(BF16)
    slope = sig * (1.0 + pre * (1.0 - sig))
    pre_grad = (cot[...].astype(F32) * slope).astype(BF16)
    grad[...] = lax.dot_general(
        pre_grad, w, (((1,), (1,)), ((), ())), preferred_element_type=F32
    ).astype(BF16)
    wgrad[...] = lax.dot_general(
        agg, pre_grad, (((0,), (0,)), ((), ())), preferred_element_type=F32
    )


def dense(ids, recv, weight, cot):
    nodes, channels = cot.shape
    full = jax.ShapeDtypeStruct((nodes, channels), BF16)
    return kernel_call(
        dense_kernel,
        "dense_layer",
        (full, full, jax.ShapeDtypeStruct((channels, channels), F32)),
        [(SMEM, a) for a in ids] + [(VMEM, a) for a in (recv, weight, cot)],
        12,
        DENSE_FLOPS,
        [pltpu.VMEM((nodes // BLOCK, BLOCK, channels), F32)],
    )


def reply_kernel(ids, g0, r1, r2, r3, own, o1, o2, o3, held, sem):
    me_x, me_y = position()
    for k, grads in enumerate((g0, r1, r2, r3)):
        y = lax.rem(me_y - k + YN, YN)
        for i, out in enumerate((held, o1, o2, o3)):
            x = lax.rem(me_x - i + XN, XN)
            for c in range(CAP):
                block = ids[x, (me_x * YN + y) * CAP + c]
                spot = pl.multiple_of((y * CAP + c) * BLOCK, BLOCK)
                out[pl.ds(spot, BLOCK), :] = grads[block]
    store = pltpu.make_async_copy(held, own, sem)
    store.start()
    store.wait()


def reply_slots(ids, grads, blocks_dev):
    channels = grads[0].shape[1]
    out = jax.ShapeDtypeStruct((YN * CAP * BLOCK, channels), BF16)
    grads = [g.reshape(blocks_dev, BLOCK, channels) for g in grads]
    return kernel_call(
        reply_kernel,
        "slot_replies",
        (out,) * XN,
        [(SMEM, ids)] + [(VMEM, g) for g in grads],
        6,
        REPLY_FLOPS,
        [pltpu.VMEM(out.shape, BF16), pltpu.SemaphoreType.DMA],
        (HBM,) + (VMEM,) * (XN - 1),
    )


def backward_kernel(
    src, slot, cnt, b0, b1, b2, b3, vals, om2, om1, own, op1, op2, acc, ret, in_sem, out_sem
):
    per_x = YN * CAP
    me_x, _ = position()
    load = pltpu.make_async_copy(b0, ret.at[pl.ds(me_x * per_x, per_x)], in_sem)
    load.start()
    for k, back in ((1, b1), (2, b2), (3, b3)):
        x = lax.rem(me_x + k, XN)
        for j in range(per_x):
            ret[x * per_x + j] = back[pl.ds(j * BLOCK, BLOCK), :]
    load.wait()
    steps = cnt.shape[1]
    tiles_step = vals.shape[0] // steps
    acc[...] = jnp.zeros_like(acc)
    for k in range(steps):
        for t in range(tiles_step):
            block = ret[slot[t, k]]
            block = jnp.where(t < cnt[0, k], block, jnp.zeros_like(block))
            acc[k, src[t, k]] += lax.dot_general(
                vals[k * tiles_step + t],
                block,
                (((0,), (0,)), ((), ())),
                preferred_element_type=F32,
            )
    store = pltpu.make_async_copy(acc.at[HALF], own, out_sem)
    store.start()
    for k, out in ((0, om2), (1, om1), (3, op1), (4, op2)):
        for b in range(acc.shape[1]):
            out[pl.ds(b * BLOCK, BLOCK), :] = acc[k, b].astype(BF16)
    store.wait()


def backward_products(src, slot, cnt, back, vals, blocks_dev):
    nodes, channels = blocks_dev * BLOCK, back[0].shape[1]
    steps = cnt.shape[1]
    send = jax.ShapeDtypeStruct((nodes, channels), BF16)
    own = jax.ShapeDtypeStruct((blocks_dev, BLOCK, channels), F32)
    own_back = back[0].reshape(YN * CAP, BLOCK, channels)
    return kernel_call(
        backward_kernel,
        "tile_backward",
        (send, send, own, send, send),
        [(SMEM, a) for a in (src, slot, cnt)]
        + [(HBM, own_back)]
        + [(VMEM, a) for a in (*back[1:], vals)],
        12,
        BACK_FLOPS,
        [
            pltpu.VMEM((steps, blocks_dev, BLOCK, channels), F32),
            pltpu.VMEM((XN * YN * CAP, BLOCK, channels), BF16),
            pltpu.SemaphoreType.DMA,
            pltpu.SemaphoreType.DMA,
        ],
        (VMEM, VMEM, HBM, VMEM, VMEM),
    )


def final_kernel(own, r1, r2, r3, r4, out, held, sem):
    load = pltpu.make_async_copy(own, held, sem)
    load.start()
    load.wait()
    for b in range(held.shape[0]):
        spot = pl.ds(b * BLOCK, BLOCK)
        total = held[b]
        for r in (r1, r2, r3, r4):
            total = total + r[spot, :].astype(F32)
        out[spot, :] = total.astype(BF16)


def final_sum(own, parts):
    return kernel_call(
        final_kernel,
        "grad_sum",
        jax.ShapeDtypeStruct(parts[0].shape, BF16),
        [(HBM, own)] + [(VMEM, a) for a in parts],
        4,
        FINAL_FLOPS,
        [pltpu.VMEM(own.shape, F32), pltpu.SemaphoreType.DMA],
    )


def spread_kernel(parts, out):
    total = parts[0]
    for i in range(1, parts.shape[0]):
        total = total + parts[i]
    for i in range(out.shape[0]):
        out[i] = total


def sum_and_spread(parts, copies):
    return kernel_call(
        spread_kernel,
        "sum_and_spread",
        jax.ShapeDtypeStruct((copies,) + parts.shape[1:], F32),
        [(VMEM, parts)],
        2,
        SPREAD_FLOPS,
    )


def summed_weight_grad(local_grad):
    channels = local_grad.shape[1]
    rows, dom = lax.axis_size("rows"), lax.axis_size("dom")
    outer = dom // INNER
    near = [[i * INNER + j for j in range(INNER)] for i in range(outer)]
    far = [[i * INNER + j for i in range(outer)] for j in range(INNER)]
    pieces = local_grad.reshape(rows, local_grad.shape[0] // rows, channels)
    piece = sum_and_spread(exchange(pieces, "rows"), INNER)
    piece = sum_and_spread(exchange(piece, "dom", near), outer)
    piece = sum_and_spread(exchange(piece, "dom", far), rows)
    return exchange(piece, "rows").reshape(local_grad.shape)


def per_device(
    features, weight, tile_values, tile_source, tile_slot, slot_block, tile_count, cotangent
):
    blocks_dev = features.shape[0] // BLOCK
    channels = features.shape[1]
    vals = tile_values.reshape(-1, BLOCK, BLOCK)
    src, slot = tile_source[0].T, tile_slot[0].T
    cnt = tile_count

    near = [dom_shift(features, -o) for o in OFFSETS]
    feats = [near[0], near[1], features, near[2], near[3]]
    feats = [f.reshape(blocks_dev, BLOCK, channels) for f in feats]
    recv = exchange(forward_products(src, slot, cnt, feats, vals), "rows")
    ids = jnp.pad(slot_block, ((0, ID_ROWS - 1), (0, LANES - slot_block.shape[1])))
    column = column_ids([ids] + [x_shift(ids, k) for k in range(1, XN)])
    all_ids = [column] + [y_shift(column, k) for k in range(1, YN)]
    activations, grad, local_grad = dense(all_ids, recv, weight, cotangent)

    grads = [grad] + [y_shift(grad, k) for k in range(1, YN)]
    reply = reply_slots(column, grads, blocks_dev)
    back = [reply[0]] + [None] * (XN - 1)
    for k in (1, 3, 2):
        back[k] = x_shift(reply[k], -k)
    terms = list(backward_products(src, slot, cnt, back, vals, blocks_dev))
    own = terms.pop(HALF)
    terms = [dom_shift(t, o) for t, o in zip(terms, OFFSETS)]
    weight_grad = summed_weight_grad(local_grad)
    feature_grad = final_sum(own, terms)
    return (activations, feature_grad, weight_grad)


def solution(mesh):
    return jax.shard_map(
        per_device,
        mesh=mesh,
        in_specs=(
            P(("dom", "rows"), None),
            P(),
            P(("dom", "rows"), None, None, None, None),
            P(("dom", "rows"), None, None),
            P(("dom", "rows"), None, None),
            P(("dom", "rows"), None),
            P(("dom", "rows"), None),
            P(("dom", "rows"), None),
        ),
        out_specs=(P(("dom", "rows"), None), P(("dom", "rows"), None), P()),
        check_vma=False,
    )
```

```python
import functools

import jax
import jax.numpy as jnp
from jax import lax
from jax.experimental import pallas as pl
from jax.experimental.pallas import tpu as pltpu
from jax.sharding import PartitionSpec as P

BLOCK = 128
HALF = 2
CAP = 2
XN = 4
YN = 4
INNER = 8
LANES = 128
ID_ROWS = 8
FORWARD_MIB = 56

OFFSETS = (-2, -1, 1, 2)
VMEM = pl.BlockSpec(memory_space=pltpu.VMEM)
HBM = pl.BlockSpec(memory_space=pltpu.HBM)
SMEM = pl.BlockSpec(memory_space=pltpu.SMEM)
BF16 = jnp.bfloat16
F32 = jnp.float32

GATHER_FLOPS = 1 << 20
DENSE_FLOPS = 1 << 28
REPLY_FLOPS = 10**10
BACK_FLOPS = 10**10
FINAL_FLOPS = 10**10
SPREAD_FLOPS = 1 << 16


def kernel_call(body, name, outs, ins, mib, flops, scratch=(), out_specs=None):
    nbytes = sum(a.size * a.dtype.itemsize for _, a in ins)
    return pl.pallas_call(
        body,
        out_shape=outs,
        in_specs=[space for space, _ in ins],
        out_specs=out_specs or jax.tree.map(lambda _: VMEM, outs),
        scratch_shapes=list(scratch),
        compiler_params=pltpu.CompilerParams(vmem_limit_bytes=mib << 20),
        cost_estimate=pl.CostEstimate(flops=flops, bytes_accessed=nbytes, transcendentals=0),
        name=name,
    )(*[a for _, a in ins])


def dom_shift(value, steps):
    count = lax.axis_size("dom")
    return lax.ppermute(value, "dom", [(i, (i + steps) % count) for i in range(count)])


def y_shift(value, steps):
    pairs = [(x * YN + y, x * YN + (y + steps) % YN) for x in range(XN) for y in range(YN)]
    return lax.ppermute(value, "rows", pairs)


def x_shift(value, steps):
    pairs = [(x * YN + y, (x + steps) % XN * YN + y) for x in range(XN) for y in range(YN)]
    return lax.ppermute(value, "rows", pairs)


X_GROUPS = [[x * YN + y for x in range(XN)] for y in range(YN)]
Y_GROUPS = [[x * YN + y for y in range(YN)] for x in range(XN)]


def exchange(value, axis, groups=None):
    return lax.all_to_all(
        value, axis, split_axis=0, concat_axis=0, tiled=True, axis_index_groups=groups
    )


def position():
    rank = lax.axis_index("rows")
    return lax.div(rank, YN), lax.rem(rank, YN)


def forward_kernel(src, slot, cnt, fm2, fm1, f0, fp1, fp2, vals, out, acc):
    acc[...] = jnp.zeros_like(acc)
    feats = (fm2, fm1, f0, fp1, fp2)
    tiles_step = vals.shape[0] // len(feats)
    for k, feat in enumerate(feats):
        for t in range(tiles_step):
            block = feat[src[t, k]]
            block = jnp.where(t < cnt[0, k], block, jnp.zeros_like(block))
            acc[slot[t, k]] += jnp.dot(
                vals[k * tiles_step + t], block, preferred_element_type=F32
            )
    for n in range(acc.shape[0]):
        out[n // CAP, pl.ds(n % CAP * BLOCK, BLOCK), :] = acc[n].astype(BF16)


def forward_products(src, slot, cnt, feats, vals):
    channels = feats[0].shape[2]
    return kernel_call(
        forward_kernel,
        "tile_forward",
        jax.ShapeDtypeStruct((XN * YN, CAP * BLOCK, channels), BF16),
        [(SMEM, a) for a in (src, slot, cnt)] + [(VMEM, a) for a in (*feats, vals)],
        FORWARD_MIB,
        vals.size * 2 * channels,
        [pltpu.VMEM((XN * YN * CAP, BLOCK, channels), F32)],
    )


def ids_kernel(own, i1, i2, i3, out):
    me_x, _ = position()
    out[...] = jnp.zeros_like(out)
    for k, ids in enumerate((own, i1, i2, i3)):
        out[pl.ds(lax.rem(me_x - k + XN, XN), 1), :] = ids[pl.ds(0, 1), :]


def column_ids(ids):
    return kernel_call(
        ids_kernel,
        "column_ids",
        jax.ShapeDtypeStruct(ids[0].shape, jnp.int32),
        [(VMEM, a) for a in ids],
        2,
        1 << 10,
    )


def dense_kernel(i0, i1, i2, i3, recv, weight, cot, act, grad, wgrad, acc):
    me_x, me_y = position()
    first = (me_x * YN + me_y) * CAP
    acc[...] = jnp.zeros_like(acc)
    for k, ids in enumerate((i0, i1, i2, i3)):
        y = lax.rem(me_y - k + YN, YN)
        for x in range(XN):
            for c in range(CAP):
                part = recv[x * YN + y, pl.ds(c * BLOCK, BLOCK), :]
                acc[ids[x, first + c]] += part.astype(F32)
    agg = acc[...].reshape(cot.shape).astype(BF16)
    w = weight[...]
    pre = jnp.dot(agg, w, preferred_element_type=F32)
    sig = 1.0 / (1.0 + jnp.exp(-pre))
    act[...] = (pre * sig).astype(BF16)
    slope = sig * (1.0 + pre * (1.0 - sig))
    pre_grad = (cot[...].astype(F32) * slope).astype(BF16)
    grad[...] = lax.dot_general(
        pre_grad, w, (((1,), (1,)), ((), ())), preferred_element_type=F32
    ).astype(BF16)
    wgrad[...] = lax.dot_general(
        agg, pre_grad, (((0,), (0,)), ((), ())), preferred_element_type=F32
    ).astype(BF16)


def dense(ids, recv, weight, cot):
    nodes, channels = cot.shape
    full = jax.ShapeDtypeStruct((nodes, channels), BF16)
    return kernel_call(
        dense_kernel,
        "dense_layer",
        (full, full, jax.ShapeDtypeStruct((channels, channels), BF16)),
        [(SMEM, a) for a in ids] + [(VMEM, a) for a in (recv, weight, cot)],
        12,
        DENSE_FLOPS,
        [pltpu.VMEM((nodes // BLOCK, BLOCK, channels), F32)],
    )


def reply_kernel(ids, g0, r1, r2, r3, own, o1, o2, o3, held, sem):
    me_x, me_y = position()
    for k, grads in enumerate((g0, r1, r2, r3)):
        y = lax.rem(me_y - k + YN, YN)
        for i, out in enumerate((held, o1, o2, o3)):
            x = lax.rem(me_x - i + XN, XN)
            for c in range(CAP):
                block = ids[x, (me_x * YN + y) * CAP + c]
                spot = pl.multiple_of((y * CAP + c) * BLOCK, BLOCK)
                out[pl.ds(spot, BLOCK), :] = grads[block]
    store = pltpu.make_async_copy(held, own, sem)
    store.start()
    store.wait()


def reply_slots(ids, grads, blocks_dev):
    channels = grads[0].shape[1]
    out = jax.ShapeDtypeStruct((YN * CAP * BLOCK, channels), BF16)
    grads = [g.reshape(blocks_dev, BLOCK, channels) for g in grads]
    return kernel_call(
        reply_kernel,
        "slot_replies",
        (out,) * XN,
        [(SMEM, ids)] + [(VMEM, g) for g in grads],
        6,
        REPLY_FLOPS,
        [pltpu.VMEM(out.shape, BF16), pltpu.SemaphoreType.DMA],
        (HBM,) + (VMEM,) * (XN - 1),
    )


def backward_kernel(
    src, slot, cnt, b0, b1, b2, b3, vals, om2, om1, own, op1, op2, acc, ret, in_sem, out_sem
):
    per_x = YN * CAP
    me_x, _ = position()
    load = pltpu.make_async_copy(b0, ret.at[pl.ds(me_x * per_x, per_x)], in_sem)
    load.start()
    for k, back in ((1, b1), (2, b2), (3, b3)):
        x = lax.rem(me_x + k, XN)
        for j in range(per_x):
            ret[x * per_x + j] = back[pl.ds(j * BLOCK, BLOCK), :]
    load.wait()
    steps = cnt.shape[1]
    tiles_step = vals.shape[0] // steps
    acc[...] = jnp.zeros_like(acc)
    for k in range(steps):
        for t in range(tiles_step):
            block = ret[slot[t, k]]
            block = jnp.where(t < cnt[0, k], block, jnp.zeros_like(block))
            acc[k, src[t, k]] += lax.dot_general(
                vals[k * tiles_step + t],
                block,
                (((0,), (0,)), ((), ())),
                preferred_element_type=F32,
            )
    store = pltpu.make_async_copy(acc.at[HALF], own, out_sem)
    store.start()
    for k, out in ((0, om2), (1, om1), (3, op1), (4, op2)):
        for b in range(acc.shape[1]):
            out[pl.ds(b * BLOCK, BLOCK), :] = acc[k, b].astype(BF16)
    store.wait()


def backward_products(src, slot, cnt, back, vals, blocks_dev):
    nodes, channels = blocks_dev * BLOCK, back[0].shape[1]
    steps = cnt.shape[1]
    send = jax.ShapeDtypeStruct((nodes, channels), BF16)
    own = jax.ShapeDtypeStruct((blocks_dev, BLOCK, channels), F32)
    own_back = back[0].reshape(YN * CAP, BLOCK, channels)
    return kernel_call(
        backward_kernel,
        "tile_backward",
        (send, send, own, send, send),
        [(SMEM, a) for a in (src, slot, cnt)]
        + [(HBM, own_back)]
        + [(VMEM, a) for a in (*back[1:], vals)],
        12,
        BACK_FLOPS,
        [
            pltpu.VMEM((steps, blocks_dev, BLOCK, channels), F32),
            pltpu.VMEM((XN * YN * CAP, BLOCK, channels), BF16),
            pltpu.SemaphoreType.DMA,
            pltpu.SemaphoreType.DMA,
        ],
        (VMEM, VMEM, HBM, VMEM, VMEM),
    )


def final_kernel(own, r1, r2, r3, r4, out, held, sem):
    load = pltpu.make_async_copy(own, held, sem)
    load.start()
    load.wait()
    for b in range(held.shape[0]):
        spot = pl.ds(b * BLOCK, BLOCK)
        total = held[b]
        for r in (r1, r2, r3, r4):
            total = total + r[spot, :].astype(F32)
        out[spot, :] = total.astype(BF16)


def final_sum(own, parts):
    return kernel_call(
        final_kernel,
        "grad_sum",
        jax.ShapeDtypeStruct(parts[0].shape, BF16),
        [(HBM, own)] + [(VMEM, a) for a in parts],
        4,
        FINAL_FLOPS,
        [pltpu.VMEM(own.shape, F32), pltpu.SemaphoreType.DMA],
    )


def spread_kernel(parts, out):
    total = parts[0].astype(F32)
    for i in range(1, parts.shape[0]):
        total = total + parts[i].astype(F32)
    for i in range(out.shape[0]):
        out[i] = total.astype(out.dtype)


def sum_and_spread(parts, copies, dtype=F32):
    return kernel_call(
        spread_kernel,
        "sum_and_spread",
        jax.ShapeDtypeStruct((copies,) + parts.shape[1:], dtype),
        [(VMEM, parts)],
        2,
        SPREAD_FLOPS,
    )


def summed_weight_grad(local_grad):
    channels = local_grad.shape[1]
    rows, dom = lax.axis_size("rows"), lax.axis_size("dom")
    outer = dom // INNER
    near = [[i * INNER + j for j in range(INNER)] for i in range(outer)]
    far = [[i * INNER + j for i in range(outer)] for j in range(INNER)]
    pieces = local_grad.reshape(rows, local_grad.shape[0] // rows, channels)
    piece = sum_and_spread(exchange(pieces, "rows"), INNER)
    piece = sum_and_spread(exchange(piece, "dom", near), outer)
    piece = sum_and_spread(exchange(piece, "dom", far), rows, BF16)
    return exchange(piece, "rows").reshape(local_grad.shape).astype(F32)


def per_device(
    features, weight, tile_values, tile_source, tile_slot, slot_block, tile_count, cotangent
):
    blocks_dev = features.shape[0] // BLOCK
    channels = features.shape[1]
    vals = tile_values.reshape(-1, BLOCK, BLOCK)
    src, slot = tile_source[0].T, tile_slot[0].T
    cnt = tile_count

    near = [dom_shift(features, -o) for o in OFFSETS]
    feats = [near[0], near[1], features, near[2], near[3]]
    feats = [f.reshape(blocks_dev, BLOCK, channels) for f in feats]
    recv = exchange(forward_products(src, slot, cnt, feats, vals), "rows")
    ids = jnp.pad(slot_block, ((0, ID_ROWS - 1), (0, LANES - slot_block.shape[1])))
    column = column_ids([ids] + [x_shift(ids, k) for k in range(1, XN)])
    all_ids = [column] + [y_shift(column, k) for k in range(1, YN)]
    activations, grad, local_grad = dense(all_ids, recv, weight, cotangent)

    grads = [grad] + [y_shift(grad, k) for k in range(1, YN)]
    reply = reply_slots(column, grads, blocks_dev)
    back = [reply[0]] + [None] * (XN - 1)
    for k in (1, 3, 2):
        back[k] = x_shift(reply[k], -k)
    terms = list(backward_products(src, slot, cnt, back, vals, blocks_dev))
    own = terms.pop(HALF)
    terms = [dom_shift(t, o) for t, o in zip(terms, OFFSETS)]
    weight_grad = summed_weight_grad(local_grad)
    feature_grad = final_sum(own, terms)
    return (activations, feature_grad, weight_grad)


def solution(mesh):
    return jax.shard_map(
        per_device,
        mesh=mesh,
        in_specs=(
            P(("dom", "rows"), None),
            P(),
            P(("dom", "rows"), None, None, None, None),
            P(("dom", "rows"), None, None),
            P(("dom", "rows"), None, None),
            P(("dom", "rows"), None),
            P(("dom", "rows"), None),
            P(("dom", "rows"), None),
        ),
        out_specs=(P(("dom", "rows"), None), P(("dom", "rows"), None), P()),
        check_vma=False,
    )
```

```python
import functools

import jax
import jax.numpy as jnp
from jax import lax
from jax.experimental import pallas as pl
from jax.experimental.pallas import tpu as pltpu
from jax.sharding import PartitionSpec as P

BLOCK = 128
HALF = 2
CAP = 2
XN = 4
YN = 4
INNER = 8
LANES = 128
ID_ROWS = 16
FORWARD_MIB = 56

OFFSETS = (-2, -1, 1, 2)
VMEM = pl.BlockSpec(memory_space=pltpu.VMEM)
HBM = pl.BlockSpec(memory_space=pltpu.HBM)
ANY = pl.BlockSpec(memory_space=pl.ANY)
SMEM = pl.BlockSpec(memory_space=pltpu.SMEM)
BF16 = jnp.bfloat16
F32 = jnp.float32

GATHER_FLOPS = 10**11
DENSE_FLOPS = 1 << 28
REPLY_FLOPS = 10**10
BACK_FLOPS = 10**10
FINAL_FLOPS = 10**10
SPREAD_FLOPS = 1 << 16


def kernel_call(body, name, outs, ins, mib, flops, scratch=(), out_specs=None):
    nbytes = sum(a.size * a.dtype.itemsize for _, a in ins)
    return pl.pallas_call(
        body,
        out_shape=outs,
        in_specs=[space for space, _ in ins],
        out_specs=out_specs or jax.tree.map(lambda _: VMEM, outs),
        scratch_shapes=list(scratch),
        compiler_params=pltpu.CompilerParams(vmem_limit_bytes=mib << 20),
        cost_estimate=pl.CostEstimate(flops=flops, bytes_accessed=nbytes, transcendentals=0),
        name=name,
    )(*[a for _, a in ins])


def dom_shift(value, steps):
    count = lax.axis_size("dom")
    return lax.ppermute(value, "dom", [(i, (i + steps) % count) for i in range(count)])


def y_shift(value, steps):
    pairs = [(x * YN + y, x * YN + (y + steps) % YN) for x in range(XN) for y in range(YN)]
    return lax.ppermute(value, "rows", pairs)


def x_shift(value, steps):
    pairs = [(x * YN + y, (x + steps) % XN * YN + y) for x in range(XN) for y in range(YN)]
    return lax.ppermute(value, "rows", pairs)


X_GROUPS = [[x * YN + y for x in range(XN)] for y in range(YN)]
Y_GROUPS = [[x * YN + y for y in range(YN)] for x in range(XN)]


def exchange(value, axis, groups=None):
    return lax.all_to_all(
        value, axis, split_axis=0, concat_axis=0, tiled=True, axis_index_groups=groups
    )


def position():
    rank = lax.axis_index("rows")
    return lax.div(rank, YN), lax.rem(rank, YN)


def forward_kernel(src, slot, cnt, ids, fm2, fm1, f0, fp1, fp2, vals, *refs):
    outs, acc = refs[:-1], refs[-1]
    acc[...] = jnp.zeros_like(acc)
    feats = (fm2, fm1, f0, fp1, fp2)
    tiles_step = vals.shape[0] // len(feats)
    for k, feat in enumerate(feats):
        for t in range(tiles_step):
            block = feat[src[t, k]]
            block = jnp.where(t < cnt[0, k], block, jnp.zeros_like(block))
            acc[slot[t, k]] += jnp.dot(
                vals[k * tiles_step + t], block, preferred_element_type=F32
            )
    me_x, _ = position()
    per_x = YN * CAP
    line = lax.broadcasted_iota(jnp.int32, (ID_ROWS, LANES), 0)
    for k in range(XN):
        x = lax.rem(me_x + k, XN)
        rows = jnp.zeros_like(line)
        for j in range(per_x):
            total = acc[x * per_x + j].astype(BF16)
            rows = jnp.where(line == j, ids[0, x * per_x + j], rows)
            for h in range(2):
                part = total[:, h * LANES : (h + 1) * LANES]
                outs[h * XN + k][pl.ds(j * BLOCK, BLOCK), :] = part
        outs[k][pl.ds(per_x * BLOCK, ID_ROWS), :] = rows.astype(F32).astype(BF16)


def forward_products(src, slot, cnt, feats, vals, ids):
    rows = YN * CAP * BLOCK
    first = jax.ShapeDtypeStruct((rows + ID_ROWS, LANES), BF16)
    second = jax.ShapeDtypeStruct((rows, LANES), BF16)
    return kernel_call(
        forward_kernel,
        "tile_forward",
        (first,) * XN + (second,) * XN,
        [(SMEM, a) for a in (src, slot, cnt, ids)] + [(VMEM, a) for a in (*feats, vals)],
        FORWARD_MIB,
        vals.size * 4 * LANES,
        [pltpu.VMEM((XN * YN * CAP, BLOCK, 2 * LANES), F32)],
    )


def gather_kernel(blocks_dev, recv, ids, outs):
    _, me_y = position()
    chunk = 64
    for i, out in enumerate(outs):
        y = lax.rem(me_y + i, YN)
        rows = {}
        for k in range(XN):
            for c in range(CAP):
                rows[k, c] = ids[pl.ds(k * YN * CAP + y * CAP + c, 1), :][:, :LANES]
        for start in range(0, BLOCK, chunk):
            totals = [jnp.zeros((chunk, LANES), F32) for _ in range(blocks_dev)]
            for (k, c), row in rows.items():
                spot = pl.multiple_of((y * CAP + c) * BLOCK + start, chunk)
                part = recv[k][pl.ds(spot, chunk), :].astype(F32)
                for b in range(blocks_dev):
                    totals[b] = totals[b] + jnp.where(row == float(b), part, 0.0)
            for b in range(blocks_dev):
                out[pl.ds(b * BLOCK + start, chunk), :] = totals[b].astype(BF16)


def gather0_kernel(blocks_dev, *refs):
    recv, outs, ids = refs[:XN], refs[XN:-1], refs[-1]
    per_x = YN * CAP
    for k in range(XN):
        got = recv[k][pl.ds(per_x * BLOCK, ID_ROWS), :].astype(F32)[:per_x]
        ids[pl.ds(k * per_x, per_x), :] = jnp.concatenate([got, got], axis=1)
    gather_kernel(blocks_dev, recv, ids, outs)


def gather1_kernel(blocks_dev, *refs):
    gather_kernel(blocks_dev, refs[:XN], refs[XN], refs[XN + 1 :])


def gather_blocks(recv, blocks_dev, ids=None):
    outs = (jax.ShapeDtypeStruct((blocks_dev * BLOCK, LANES), BF16),) * YN
    if ids is None:
        outs += (jax.ShapeDtypeStruct((XN * YN * CAP, 2 * LANES), F32),)
    return kernel_call(
        functools.partial(gather0_kernel if ids is None else gather1_kernel, blocks_dev),
        "block_sums",
        outs,
        [(VMEM, a) for a in recv] + ([] if ids is None else [(VMEM, ids)]),
        6,
        GATHER_FLOPS,
    )


def dense_kernel(*refs):
    parts, (weight, cot, act, grad, wgrad) = refs[: 2 * YN], refs[2 * YN :]
    halves = []
    for h in range(2):
        total = parts[h * YN][...].astype(F32)
        for k in range(1, YN):
            total = total + parts[h * YN + k][...].astype(F32)
        halves.append(total.astype(BF16))
    agg = jnp.concatenate(halves, axis=1)
    w = weight[...]
    pre = jnp.dot(agg, w, preferred_element_type=F32)
    sig = 1.0 / (1.0 + jnp.exp(-pre))
    act[...] = (pre * sig).astype(BF16)
    slope = sig * (1.0 + pre * (1.0 - sig))
    pre_grad = (cot[...].astype(F32) * slope).astype(BF16)
    grad[...] = lax.dot_general(
        pre_grad, w, (((1,), (1,)), ((), ())), preferred_element_type=F32
    ).astype(BF16)
    wgrad[...] = lax.dot_general(
        agg, pre_grad, (((0,), (0,)), ((), ())), preferred_element_type=F32
    ).astype(BF16)


def dense(parts, weight, cot):
    nodes, channels = cot.shape
    full = jax.ShapeDtypeStruct((nodes, channels), BF16)
    return kernel_call(
        dense_kernel,
        "dense_layer",
        (full, full, jax.ShapeDtypeStruct((channels, channels), BF16)),
        [(VMEM, a) for a in (*parts, weight, cot)],
        10,
        DENSE_FLOPS,
    )


def reply_kernel(ids, g0, r1, r2, r3, own, o1, o2, o3, held, sem):
    _, me_y = position()
    chunk = 32
    for k, grads in enumerate((g0, r1, r2, r3)):
        y = lax.rem(me_y - k + YN, YN)
        rows = {}
        for i in range(XN):
            for c in range(CAP):
                rows[i, c] = ids[pl.ds(i * YN * CAP + y * CAP + c, 1), :]
        for start in range(0, BLOCK, chunk):
            blocks = [grads[b, pl.ds(start, chunk), :].astype(F32) for b in range(grads.shape[0])]
            for (i, c), row in rows.items():
                picked = jnp.where(row == 0.0, blocks[0], 0.0)
                for b in range(1, len(blocks)):
                    picked = jnp.where(row == float(b), blocks[b], picked)
                spot = pl.multiple_of((y * CAP + c) * BLOCK + start, chunk)
                (held, o1, o2, o3)[i][pl.ds(spot, chunk), :] = picked.astype(BF16)
    store = pltpu.make_async_copy(held, own, sem)
    store.start()
    store.wait()


def reply_slots(ids, grads, blocks_dev):
    channels = grads[0].shape[1]
    out = jax.ShapeDtypeStruct((YN * CAP * BLOCK, channels), BF16)
    grads = [g.reshape(blocks_dev, BLOCK, channels) for g in grads]
    return kernel_call(
        reply_kernel,
        "slot_replies",
        (out,) * XN,
        [(VMEM, a) for a in (ids, *grads)],
        6,
        REPLY_FLOPS,
        [pltpu.VMEM(out.shape, BF16), pltpu.SemaphoreType.DMA],
        (HBM,) + (VMEM,) * (XN - 1),
    )


def backward_kernel(
    src, slot, cnt, after, b0, b1, b2, b3, vals, om2, om1, own, op1, op2, acc, ret, in_sem, out_sem
):
    per_x = YN * CAP
    me_x, _ = position()
    load = pltpu.make_async_copy(b0, ret.at[pl.ds(me_x * per_x, per_x)], in_sem)
    load.start()
    for k, back in ((1, b1), (2, b2), (3, b3)):
        x = lax.rem(me_x + k, XN)
        for j in range(per_x):
            ret[x * per_x + j] = back[pl.ds(j * BLOCK, BLOCK), :]
    load.wait()
    steps = cnt.shape[1]
    tiles_step = vals.shape[0] // steps
    acc[...] = jnp.zeros_like(acc)
    for k in range(steps):
        for t in range(tiles_step):
            block = ret[slot[t, k]]
            block = jnp.where(t < cnt[0, k], block, jnp.zeros_like(block))
            acc[k, src[t, k]] += lax.dot_general(
                vals[k * tiles_step + t],
                block,
                (((0,), (0,)), ((), ())),
                preferred_element_type=F32,
            )
    store = pltpu.make_async_copy(acc.at[HALF], own, out_sem)
    store.start()
    for k, out in ((0, om2), (1, om1), (3, op1), (4, op2)):
        for b in range(acc.shape[1]):
            out[pl.ds(b * BLOCK, BLOCK), :] = acc[k, b].astype(BF16)
    store.wait()


def backward_products(src, slot, cnt, back, vals, blocks_dev, after):
    nodes, channels = blocks_dev * BLOCK, back[0].shape[1]
    steps = cnt.shape[1]
    send = jax.ShapeDtypeStruct((nodes, channels), BF16)
    own = jax.ShapeDtypeStruct((blocks_dev, BLOCK, channels), F32)
    own_back = back[0].reshape(YN * CAP, BLOCK, channels)
    return kernel_call(
        backward_kernel,
        "tile_backward",
        (send, send, own, send, send),
        [(SMEM, a) for a in (src, slot, cnt)]
        + [(ANY, after), (HBM, own_back)]
        + [(VMEM, a) for a in (*back[1:], vals)],
        12,
        BACK_FLOPS,
        [
            pltpu.VMEM((steps, blocks_dev, BLOCK, channels), F32),
            pltpu.VMEM((XN * YN * CAP, BLOCK, channels), BF16),
            pltpu.SemaphoreType.DMA,
            pltpu.SemaphoreType.DMA,
        ],
        (VMEM, VMEM, HBM, VMEM, VMEM),
    )


def final_kernel(own, r1, r2, r3, r4, out, held, sem):
    load = pltpu.make_async_copy(own, held, sem)
    load.start()
    load.wait()
    for b in range(held.shape[0]):
        spot = pl.ds(b * BLOCK, BLOCK)
        total = held[b]
        for r in (r1, r2, r3, r4):
            total = total + r[spot, :].astype(F32)
        out[spot, :] = total.astype(BF16)


def final_sum(own, parts):
    return kernel_call(
        final_kernel,
        "grad_sum",
        jax.ShapeDtypeStruct(parts[0].shape, BF16),
        [(HBM, own)] + [(VMEM, a) for a in parts],
        4,
        FINAL_FLOPS,
        [pltpu.VMEM(own.shape, F32), pltpu.SemaphoreType.DMA],
    )


def spread_kernel(parts, out):
    total = parts[0].astype(F32)
    for i in range(1, parts.shape[0]):
        total = total + parts[i].astype(F32)
    for i in range(out.shape[0]):
        out[i] = total.astype(out.dtype)


def sum_and_spread(parts, copies, dtype=F32):
    return kernel_call(
        spread_kernel,
        "sum_and_spread",
        jax.ShapeDtypeStruct((copies,) + parts.shape[1:], dtype),
        [(VMEM, parts)],
        2,
        SPREAD_FLOPS,
    )


def weight_piece(local_grad):
    rows, dom = lax.axis_size("rows"), lax.axis_size("dom")
    outer = dom // INNER
    near = [[i * INNER + j for j in range(INNER)] for i in range(outer)]
    far = [[i * INNER + j for i in range(outer)] for j in range(INNER)]
    pieces = local_grad.reshape(rows, local_grad.shape[0] // rows, local_grad.shape[1])
    piece = sum_and_spread(exchange(pieces, "rows"), INNER)
    piece = sum_and_spread(exchange(piece, "dom", near), outer)
    return sum_and_spread(exchange(piece, "dom", far), rows, BF16)


def per_device(
    features, weight, tile_values, tile_source, tile_slot, slot_block, tile_count, cotangent
):
    blocks_dev = features.shape[0] // BLOCK
    channels = features.shape[1]
    vals = tile_values.reshape(-1, BLOCK, BLOCK)
    src, slot = tile_source[0].T, tile_slot[0].T
    cnt = tile_count

    near = [dom_shift(features, -o) for o in OFFSETS]
    feats = [near[0], near[1], features, near[2], near[3]]
    feats = [f.reshape(blocks_dev, BLOCK, channels) for f in feats]
    sent = forward_products(src, slot, cnt, feats, vals, slot_block)
    got0 = [sent[0]] + [x_shift(sent[k], k) for k in range(1, XN)]
    got1 = [sent[XN]] + [x_shift(sent[XN + k], k) for k in range(1, XN)]
    *sums0, ids = gather_blocks(got0, blocks_dev)
    parts = [sums0[0]] + [y_shift(sums0[k], k) for k in range(1, YN)]
    sums1 = gather_blocks(got1, blocks_dev, ids)
    parts += [sums1[0]] + [y_shift(sums1[k], k) for k in range(1, YN)]
    activations, grad, local_grad = dense(parts, weight, cotangent)

    piece = weight_piece(local_grad)
    grads = [grad] + [y_shift(grad, k) for k in range(1, YN)]
    reply = reply_slots(ids, grads, blocks_dev)
    back = [reply[0]] + [None] * (XN - 1)
    for k in (1, 3, 2):
        back[k] = x_shift(reply[k], -k)
    terms = list(backward_products(src, slot, cnt, back, vals, blocks_dev, piece))
    own = terms.pop(HALF)
    terms = [dom_shift(t, o) for t, o in zip(terms, OFFSETS)]
    weight_grad = exchange(piece, "rows").reshape(local_grad.shape).astype(F32)
    feature_grad = final_sum(own, terms)
    return (activations, feature_grad, weight_grad)


def solution(mesh):
    return jax.shard_map(
        per_device,
        mesh=mesh,
        in_specs=(
            P(("dom", "rows"), None),
            P(),
            P(("dom", "rows"), None, None, None, None),
            P(("dom", "rows"), None, None),
            P(("dom", "rows"), None, None),
            P(("dom", "rows"), None),
            P(("dom", "rows"), None),
            P(("dom", "rows"), None),
        ),
        out_specs=(P(("dom", "rows"), None), P(("dom", "rows"), None), P()),
        check_vma=False,
    )
```

```python
import functools

import jax
import jax.numpy as jnp
from jax import lax
from jax.experimental import pallas as pl
from jax.experimental.pallas import tpu as pltpu
from jax.sharding import PartitionSpec as P

BLOCK = 128
HALF = 2
CAP = 2
XN = 4
YN = 4
INNER = 8
LANES = 128
ID_ROWS = 16
FORWARD_MIB = 56

OFFSETS = (-2, -1, 1, 2)
VMEM = pl.BlockSpec(memory_space=pltpu.VMEM)
HBM = pl.BlockSpec(memory_space=pltpu.HBM)
SMEM = pl.BlockSpec(memory_space=pltpu.SMEM)
BF16 = jnp.bfloat16
F32 = jnp.float32

GATHER_FLOPS = 10**11
DENSE_FLOPS = 1 << 28
REPLY_FLOPS = 10**10
BACK_FLOPS = 10**10
FINAL_FLOPS = 10**10
SPREAD_FLOPS = 1 << 16


def kernel_call(body, name, outs, ins, mib, flops, scratch=(), out_specs=None):
    nbytes = sum(a.size * a.dtype.itemsize for _, a in ins)
    return pl.pallas_call(
        body,
        out_shape=outs,
        in_specs=[space for space, _ in ins],
        out_specs=out_specs or jax.tree.map(lambda _: VMEM, outs),
        scratch_shapes=list(scratch),
        compiler_params=pltpu.CompilerParams(vmem_limit_bytes=mib << 20),
        cost_estimate=pl.CostEstimate(flops=flops, bytes_accessed=nbytes, transcendentals=0),
        name=name,
    )(*[a for _, a in ins])


def dom_shift(value, steps):
    count = lax.axis_size("dom")
    return lax.ppermute(value, "dom", [(i, (i + steps) % count) for i in range(count)])


def y_shift(value, steps):
    pairs = [(x * YN + y, x * YN + (y + steps) % YN) for x in range(XN) for y in range(YN)]
    return lax.ppermute(value, "rows", pairs)


def x_shift(value, steps):
    pairs = [(x * YN + y, (x + steps) % XN * YN + y) for x in range(XN) for y in range(YN)]
    return lax.ppermute(value, "rows", pairs)


X_GROUPS = [[x * YN + y for x in range(XN)] for y in range(YN)]
Y_GROUPS = [[x * YN + y for y in range(YN)] for x in range(XN)]


def exchange(value, axis, groups=None):
    return lax.all_to_all(
        value, axis, split_axis=0, concat_axis=0, tiled=True, axis_index_groups=groups
    )


def position():
    rank = lax.axis_index("rows")
    return lax.div(rank, YN), lax.rem(rank, YN)


def forward_kernel(src, slot, cnt, ids, fm2, fm1, f0, fp1, fp2, vals, *refs):
    outs, acc = refs[:-1], refs[-1]
    acc[...] = jnp.zeros_like(acc)
    feats = (fm2, fm1, f0, fp1, fp2)
    tiles_step = vals.shape[0] // len(feats)
    for k, feat in enumerate(feats):
        for t in range(tiles_step):
            block = feat[src[t, k]]
            block = jnp.where(t < cnt[0, k], block, jnp.zeros_like(block))
            acc[slot[t, k]] += jnp.dot(
                vals[k * tiles_step + t], block, preferred_element_type=F32
            )
    me_x, _ = position()
    per_x = YN * CAP
    line = lax.broadcasted_iota(jnp.int32, (ID_ROWS, LANES), 0)
    for k in range(XN):
        x = lax.rem(me_x + k, XN)
        rows = jnp.zeros_like(line)
        for j in range(per_x):
            total = acc[x * per_x + j].astype(BF16)
            rows = jnp.where(line == j, ids[0, x * per_x + j], rows)
            for h in range(2):
                part = total[:, h * LANES : (h + 1) * LANES]
                outs[h * XN + k][pl.ds(j * BLOCK, BLOCK), :] = part
        outs[k][pl.ds(per_x * BLOCK, ID_ROWS), :] = rows.astype(F32).astype(BF16)


def forward_products(src, slot, cnt, feats, vals, ids):
    rows = YN * CAP * BLOCK
    first = jax.ShapeDtypeStruct((rows + ID_ROWS, LANES), BF16)
    second = jax.ShapeDtypeStruct((rows, LANES), BF16)
    return kernel_call(
        forward_kernel,
        "tile_forward",
        (first,) * XN + (second,) * XN,
        [(SMEM, a) for a in (src, slot, cnt, ids)] + [(VMEM, a) for a in (*feats, vals)],
        FORWARD_MIB,
        vals.size * 4 * LANES,
        [pltpu.VMEM((XN * YN * CAP, BLOCK, 2 * LANES), F32)],
    )


def gather_kernel(blocks_dev, recv, ids, outs):
    _, me_y = position()
    chunk = 64
    for i, out in enumerate(outs):
        y = lax.rem(me_y + i, YN)
        rows = {}
        for k in range(XN):
            for c in range(CAP):
                rows[k, c] = ids[pl.ds(k * YN * CAP + y * CAP + c, 1), :][:, :LANES]
        for start in range(0, BLOCK, chunk):
            totals = [jnp.zeros((chunk, LANES), F32) for _ in range(blocks_dev)]
            for (k, c), row in rows.items():
                spot = pl.multiple_of((y * CAP + c) * BLOCK + start, chunk)
                part = recv[k][pl.ds(spot, chunk), :].astype(F32)
                for b in range(blocks_dev):
                    totals[b] = totals[b] + jnp.where(row == float(b), part, 0.0)
            for b in range(blocks_dev):
                out[pl.ds(b * BLOCK + start, chunk), :] = totals[b].astype(BF16)


def gather0_kernel(blocks_dev, *refs):
    recv, outs, ids = refs[:XN], refs[XN:-1], refs[-1]
    per_x = YN * CAP
    for k in range(XN):
        got = recv[k][pl.ds(per_x * BLOCK, ID_ROWS), :].astype(F32)[:per_x]
        ids[pl.ds(k * per_x, per_x), :] = jnp.concatenate([got, got], axis=1)
    gather_kernel(blocks_dev, recv, ids, outs)


def gather1_kernel(blocks_dev, *refs):
    gather_kernel(blocks_dev, refs[:XN], refs[XN], refs[XN + 1 :])


def gather_blocks(recv, blocks_dev, ids=None):
    outs = (jax.ShapeDtypeStruct((blocks_dev * BLOCK, LANES), BF16),) * YN
    if ids is None:
        outs += (jax.ShapeDtypeStruct((XN * YN * CAP, 2 * LANES), F32),)
    return kernel_call(
        functools.partial(gather0_kernel if ids is None else gather1_kernel, blocks_dev),
        "block_sums",
        outs,
        [(VMEM, a) for a in recv] + ([] if ids is None else [(VMEM, ids)]),
        6,
        GATHER_FLOPS,
    )


def dense_kernel(*refs):
    parts, (weight, cot, act, grad, wgrad) = refs[: 2 * YN], refs[2 * YN :]
    halves = []
    for h in range(2):
        total = parts[h * YN][...].astype(F32)
        for k in range(1, YN):
            total = total + parts[h * YN + k][...].astype(F32)
        halves.append(total.astype(BF16))
    agg = jnp.concatenate(halves, axis=1)
    w = weight[...]
    pre = jnp.dot(agg, w, preferred_element_type=F32)
    sig = 1.0 / (1.0 + jnp.exp(-pre))
    act[...] = (pre * sig).astype(BF16)
    slope = sig * (1.0 + pre * (1.0 - sig))
    pre_grad = (cot[...].astype(F32) * slope).astype(BF16)
    grad[...] = lax.dot_general(
        pre_grad, w, (((1,), (1,)), ((), ())), preferred_element_type=F32
    ).astype(BF16)
    wgrad[...] = lax.dot_general(
        agg, pre_grad, (((0,), (0,)), ((), ())), preferred_element_type=F32
    ).astype(BF16)


def dense(parts, weight, cot):
    nodes, channels = cot.shape
    full = jax.ShapeDtypeStruct((nodes, channels), BF16)
    return kernel_call(
        dense_kernel,
        "dense_layer",
        (full, full, jax.ShapeDtypeStruct((channels, channels), BF16)),
        [(VMEM, a) for a in (*parts, weight, cot)],
        10,
        DENSE_FLOPS,
    )


def reply_kernel(ids, g0, r1, r2, r3, own, o1, o2, o3, held, sem):
    _, me_y = position()
    chunk = 32
    for k, grads in enumerate((g0, r1, r2, r3)):
        y = lax.rem(me_y - k + YN, YN)
        rows = {}
        for i in range(XN):
            for c in range(CAP):
                rows[i, c] = ids[pl.ds(i * YN * CAP + y * CAP + c, 1), :]
        for start in range(0, BLOCK, chunk):
            blocks = [grads[b, pl.ds(start, chunk), :].astype(F32) for b in range(grads.shape[0])]
            for (i, c), row in rows.items():
                picked = jnp.where(row == 0.0, blocks[0], 0.0)
                for b in range(1, len(blocks)):
                    picked = jnp.where(row == float(b), blocks[b], picked)
                spot = pl.multiple_of((y * CAP + c) * BLOCK + start, chunk)
                (held, o1, o2, o3)[i][pl.ds(spot, chunk), :] = picked.astype(BF16)
    store = pltpu.make_async_copy(held, own, sem)
    store.start()
    store.wait()


def reply_slots(ids, grads, blocks_dev):
    channels = grads[0].shape[1]
    out = jax.ShapeDtypeStruct((YN * CAP * BLOCK, channels), BF16)
    grads = [g.reshape(blocks_dev, BLOCK, channels) for g in grads]
    return kernel_call(
        reply_kernel,
        "slot_replies",
        (out,) * XN,
        [(VMEM, a) for a in (ids, *grads)],
        6,
        REPLY_FLOPS,
        [pltpu.VMEM(out.shape, BF16), pltpu.SemaphoreType.DMA],
        (HBM,) + (VMEM,) * (XN - 1),
    )


def backward_kernel(
    src, slot, cnt, b0, b1, b2, b3, vals, om2, om1, own, op1, op2, acc, ret, in_sem, out_sem
):
    per_x = YN * CAP
    me_x, _ = position()
    load = pltpu.make_async_copy(b0, ret.at[pl.ds(me_x * per_x, per_x)], in_sem)
    load.start()
    for k, back in ((1, b1), (2, b2), (3, b3)):
        x = lax.rem(me_x + k, XN)
        for j in range(per_x):
            ret[x * per_x + j] = back[pl.ds(j * BLOCK, BLOCK), :]
    load.wait()
    steps = cnt.shape[1]
    tiles_step = vals.shape[0] // steps
    acc[...] = jnp.zeros_like(acc)
    for k in range(steps):
        for t in range(tiles_step):
            block = ret[slot[t, k]]
            block = jnp.where(t < cnt[0, k], block, jnp.zeros_like(block))
            acc[k, src[t, k]] += lax.dot_general(
                vals[k * tiles_step + t],
                block,
                (((0,), (0,)), ((), ())),
                preferred_element_type=F32,
            )
    store = pltpu.make_async_copy(acc.at[HALF], own, out_sem)
    store.start()
    for k, out in ((0, om2), (1, om1), (3, op1), (4, op2)):
        for b in range(acc.shape[1]):
            out[pl.ds(b * BLOCK, BLOCK), :] = acc[k, b].astype(BF16)
    store.wait()


def backward_products(src, slot, cnt, back, vals, blocks_dev):
    nodes, channels = blocks_dev * BLOCK, back[0].shape[1]
    steps = cnt.shape[1]
    send = jax.ShapeDtypeStruct((nodes, channels), BF16)
    own = jax.ShapeDtypeStruct((blocks_dev, BLOCK, channels), F32)
    own_back = back[0].reshape(YN * CAP, BLOCK, channels)
    return kernel_call(
        backward_kernel,
        "tile_backward",
        (send, send, own, send, send),
        [(SMEM, a) for a in (src, slot, cnt)]
        + [(HBM, own_back)]
        + [(VMEM, a) for a in (*back[1:], vals)],
        12,
        BACK_FLOPS,
        [
            pltpu.VMEM((steps, blocks_dev, BLOCK, channels), F32),
            pltpu.VMEM((XN * YN * CAP, BLOCK, channels), BF16),
            pltpu.SemaphoreType.DMA,
            pltpu.SemaphoreType.DMA,
        ],
        (VMEM, VMEM, HBM, VMEM, VMEM),
    )


def final_kernel(own, r1, r2, r3, r4, out, held, sem):
    load = pltpu.make_async_copy(own, held, sem)
    load.start()
    load.wait()
    for b in range(held.shape[0]):
        spot = pl.ds(b * BLOCK, BLOCK)
        total = held[b]
        for r in (r1, r2, r3, r4):
            total = total + r[spot, :].astype(F32)
        out[spot, :] = total.astype(BF16)


def final_sum(own, parts):
    return kernel_call(
        final_kernel,
        "grad_sum",
        jax.ShapeDtypeStruct(parts[0].shape, BF16),
        [(HBM, own)] + [(VMEM, a) for a in parts],
        4,
        FINAL_FLOPS,
        [pltpu.VMEM(own.shape, F32), pltpu.SemaphoreType.DMA],
    )


def spread_kernel(parts, out):
    total = parts[0].astype(F32)
    for i in range(1, parts.shape[0]):
        total = total + parts[i].astype(F32)
    for i in range(out.shape[0]):
        out[i] = total.astype(out.dtype)


def sum_and_spread(parts, copies, dtype=F32):
    return kernel_call(
        spread_kernel,
        "sum_and_spread",
        jax.ShapeDtypeStruct((copies,) + parts.shape[1:], dtype),
        [(VMEM, parts)],
        2,
        SPREAD_FLOPS,
    )


def weight_piece(local_grad):
    rows, dom = lax.axis_size("rows"), lax.axis_size("dom")
    outer = dom // INNER
    near = [[i * INNER + j for j in range(INNER)] for i in range(outer)]
    far = [[i * INNER + j for i in range(outer)] for j in range(INNER)]
    pieces = local_grad.reshape(rows, local_grad.shape[0] // rows, local_grad.shape[1])
    piece = sum_and_spread(exchange(pieces, "rows"), INNER)
    piece = sum_and_spread(exchange(piece, "dom", near), outer)
    return sum_and_spread(exchange(piece, "dom", far), rows, BF16)


def per_device(
    features, weight, tile_values, tile_source, tile_slot, slot_block, tile_count, cotangent
):
    blocks_dev = features.shape[0] // BLOCK
    channels = features.shape[1]
    vals = tile_values.reshape(-1, BLOCK, BLOCK)
    src, slot = tile_source[0].T, tile_slot[0].T
    cnt = tile_count

    near = [dom_shift(features, -o) for o in OFFSETS]
    feats = [near[0], near[1], features, near[2], near[3]]
    feats = [f.reshape(blocks_dev, BLOCK, channels) for f in feats]
    sent = forward_products(src, slot, cnt, feats, vals, slot_block)
    got0 = [sent[0]] + [x_shift(sent[k], k) for k in range(1, XN)]
    got1 = [sent[XN]] + [x_shift(sent[XN + k], k) for k in range(1, XN)]
    *sums0, ids = gather_blocks(got0, blocks_dev)
    parts = [sums0[0]] + [y_shift(sums0[k], k) for k in range(1, YN)]
    sums1 = gather_blocks(got1, blocks_dev, ids)
    parts += [sums1[0]] + [y_shift(sums1[k], k) for k in range(1, YN)]
    activations, grad, local_grad = dense(parts, weight, cotangent)

    piece = weight_piece(local_grad)
    grads = [grad] + [y_shift(grad, k) for k in range(1, YN)]
    reply = reply_slots(ids, grads, blocks_dev)
    back = [reply[0]] + [None] * (XN - 1)
    for k in (1, 3, 2):
        back[k] = x_shift(reply[k], -k)
    terms = list(backward_products(src, slot, cnt, back, vals, blocks_dev))
    own = terms.pop(HALF)
    terms = [dom_shift(t, o) for t, o in zip(terms, OFFSETS)]
    weight_grad = exchange(piece, "rows").reshape(local_grad.shape).astype(F32)
    feature_grad = final_sum(own, terms)
    return (activations, feature_grad, weight_grad)


def solution(mesh):
    return jax.shard_map(
        per_device,
        mesh=mesh,
        in_specs=(
            P(("dom", "rows"), None),
            P(),
            P(("dom", "rows"), None, None, None, None),
            P(("dom", "rows"), None, None),
            P(("dom", "rows"), None, None),
            P(("dom", "rows"), None),
            P(("dom", "rows"), None),
            P(("dom", "rows"), None),
        ),
        out_specs=(P(("dom", "rows"), None), P(("dom", "rows"), None), P()),
        check_vma=False,
    )
```

```python
import functools

import jax
import jax.numpy as jnp
from jax import lax
from jax.experimental import pallas as pl
from jax.experimental.pallas import tpu as pltpu
from jax.sharding import PartitionSpec as P

BLOCK = 128
HALF = 2
CAP = 2
XN = 4
YN = 4
INNER = 8
LANES = 128
ID_ROWS = 16
FORWARD_MIB = 56

OFFSETS = (-2, -1, 1, 2)
VMEM = pl.BlockSpec(memory_space=pltpu.VMEM)
HBM = pl.BlockSpec(memory_space=pltpu.HBM)
SMEM = pl.BlockSpec(memory_space=pltpu.SMEM)
BF16 = jnp.bfloat16
F32 = jnp.float32

GATHER_FLOPS = 10**11
HALF_FLOPS = 10**10
DENSE_FLOPS = 1 << 28
REPLY_FLOPS = 10**10
BACK_FLOPS = 10**10
FINAL_FLOPS = 10**10
SPREAD_FLOPS = 1 << 16


def kernel_call(body, name, outs, ins, mib, flops, scratch=(), out_specs=None):
    nbytes = sum(a.size * a.dtype.itemsize for _, a in ins)
    return pl.pallas_call(
        body,
        out_shape=outs,
        in_specs=[space for space, _ in ins],
        out_specs=out_specs or jax.tree.map(lambda _: VMEM, outs),
        scratch_shapes=list(scratch),
        compiler_params=pltpu.CompilerParams(vmem_limit_bytes=mib << 20),
        cost_estimate=pl.CostEstimate(flops=flops, bytes_accessed=nbytes, transcendentals=0),
        name=name,
    )(*[a for _, a in ins])


def dom_shift(value, steps):
    count = lax.axis_size("dom")
    return lax.ppermute(value, "dom", [(i, (i + steps) % count) for i in range(count)])


def y_shift(value, steps):
    pairs = [(x * YN + y, x * YN + (y + steps) % YN) for x in range(XN) for y in range(YN)]
    return lax.ppermute(value, "rows", pairs)


def x_shift(value, steps):
    pairs = [(x * YN + y, (x + steps) % XN * YN + y) for x in range(XN) for y in range(YN)]
    return lax.ppermute(value, "rows", pairs)


X_GROUPS = [[x * YN + y for x in range(XN)] for y in range(YN)]
Y_GROUPS = [[x * YN + y for y in range(YN)] for x in range(XN)]


def exchange(value, axis, groups=None):
    return lax.all_to_all(
        value, axis, split_axis=0, concat_axis=0, tiled=True, axis_index_groups=groups
    )


def position():
    rank = lax.axis_index("rows")
    return lax.div(rank, YN), lax.rem(rank, YN)


def forward_kernel(src, slot, cnt, ids, fm2, fm1, f0, fp1, fp2, vals, *refs):
    outs, acc = refs[:-1], refs[-1]
    acc[...] = jnp.zeros_like(acc)
    feats = (fm2, fm1, f0, fp1, fp2)
    tiles_step = vals.shape[0] // len(feats)
    for k, feat in enumerate(feats):
        for t in range(tiles_step):
            block = feat[src[t, k]]
            block = jnp.where(t < cnt[0, k], block, jnp.zeros_like(block))
            acc[slot[t, k]] += jnp.dot(
                vals[k * tiles_step + t], block, preferred_element_type=F32
            )
    me_x, _ = position()
    per_x = YN * CAP
    line = lax.broadcasted_iota(jnp.int32, (ID_ROWS, LANES), 0)
    for k in range(XN):
        x = lax.rem(me_x + k, XN)
        rows = jnp.zeros_like(line)
        for j in range(per_x):
            total = acc[x * per_x + j].astype(BF16)
            rows = jnp.where(line == j, ids[0, x * per_x + j], rows)
            for h in range(2):
                part = total[:, h * LANES : (h + 1) * LANES]
                outs[h * XN + k][pl.ds(j * BLOCK, BLOCK), :] = part
        outs[k][pl.ds(per_x * BLOCK, ID_ROWS), :] = rows.astype(F32).astype(BF16)


def forward_products(src, slot, cnt, feats, vals, ids):
    rows = YN * CAP * BLOCK
    first = jax.ShapeDtypeStruct((rows + ID_ROWS, LANES), BF16)
    second = jax.ShapeDtypeStruct((rows, LANES), BF16)
    return kernel_call(
        forward_kernel,
        "tile_forward",
        (first,) * XN + (second,) * XN,
        [(SMEM, a) for a in (src, slot, cnt, ids)] + [(VMEM, a) for a in (*feats, vals)],
        FORWARD_MIB,
        vals.size * 4 * LANES,
        [pltpu.VMEM((XN * YN * CAP, BLOCK, 2 * LANES), F32)],
    )


def gather_kernel(blocks_dev, recv, ids, outs):
    _, me_y = position()
    chunk = 64
    for i, out in enumerate(outs):
        y = lax.rem(me_y + i, YN)
        rows = {}
        for k in range(XN):
            for c in range(CAP):
                rows[k, c] = ids[pl.ds(k * YN * CAP + y * CAP + c, 1), :][:, :LANES]
        for start in range(0, BLOCK, chunk):
            totals = [jnp.zeros((chunk, LANES), F32) for _ in range(blocks_dev)]
            for (k, c), row in rows.items():
                spot = pl.multiple_of((y * CAP + c) * BLOCK + start, chunk)
                part = recv[k][pl.ds(spot, chunk), :].astype(F32)
                for b in range(blocks_dev):
                    totals[b] = totals[b] + jnp.where(row == float(b), part, 0.0)
            for b in range(blocks_dev):
                out[pl.ds(b * BLOCK + start, chunk), :] = totals[b].astype(BF16)


def gather0_kernel(blocks_dev, *refs):
    recv, outs, ids = refs[:XN], refs[XN:-1], refs[-1]
    per_x = YN * CAP
    for k in range(XN):
        got = recv[k][pl.ds(per_x * BLOCK, ID_ROWS), :].astype(F32)[:per_x]
        ids[pl.ds(k * per_x, per_x), :] = jnp.concatenate([got, got], axis=1)
    gather_kernel(blocks_dev, recv, ids, outs)


def gather1_kernel(blocks_dev, *refs):
    gather_kernel(blocks_dev, refs[:XN], refs[XN], refs[XN + 1 :])


def gather_blocks(recv, blocks_dev, ids=None):
    outs = (jax.ShapeDtypeStruct((blocks_dev * BLOCK, LANES), BF16),) * YN
    if ids is None:
        outs += (jax.ShapeDtypeStruct((XN * YN * CAP, 2 * LANES), F32),)
    return kernel_call(
        functools.partial(gather0_kernel if ids is None else gather1_kernel, blocks_dev),
        "block_sums",
        outs,
        [(VMEM, a) for a in recv] + ([] if ids is None else [(VMEM, ids)]),
        6,
        GATHER_FLOPS,
    )


def summed(parts):
    total = parts[0][...].astype(F32)
    for part in parts[1:]:
        total = total + part[...].astype(F32)
    return total.astype(BF16)


def half_kernel(*refs):
    refs[-1][...] = summed(refs[:-1])


def half_sum(parts):
    return kernel_call(
        half_kernel,
        "half_sum",
        jax.ShapeDtypeStruct(parts[0].shape, BF16),
        [(VMEM, a) for a in parts],
        4,
        HALF_FLOPS,
    )


def dense_kernel(*refs):
    agg0, parts, (weight, cot, act, grad, wgrad) = refs[0], refs[1 : 1 + YN], refs[1 + YN :]
    agg = jnp.concatenate([agg0[...], summed(parts)], axis=1)
    w = weight[...]
    pre = jnp.dot(agg, w, preferred_element_type=F32)
    sig = 1.0 / (1.0 + jnp.exp(-pre))
    act[...] = (pre * sig).astype(BF16)
    slope = sig * (1.0 + pre * (1.0 - sig))
    pre_grad = (cot[...].astype(F32) * slope).astype(BF16)
    grad[...] = lax.dot_general(
        pre_grad, w, (((1,), (1,)), ((), ())), preferred_element_type=F32
    ).astype(BF16)
    wgrad[...] = lax.dot_general(
        agg, pre_grad, (((0,), (0,)), ((), ())), preferred_element_type=F32
    ).astype(BF16)


def dense(agg0, parts, weight, cot):
    nodes, channels = cot.shape
    full = jax.ShapeDtypeStruct((nodes, channels), BF16)
    return kernel_call(
        dense_kernel,
        "dense_layer",
        (full, full, jax.ShapeDtypeStruct((channels, channels), BF16)),
        [(VMEM, a) for a in (agg0, *parts, weight, cot)],
        10,
        DENSE_FLOPS,
    )


def reply_kernel(ids, g0, r1, r2, r3, own, o1, o2, o3, held, sem):
    _, me_y = position()
    chunk = 32
    for k, grads in enumerate((g0, r1, r2, r3)):
        y = lax.rem(me_y - k + YN, YN)
        rows = {}
        for i in range(XN):
            for c in range(CAP):
                rows[i, c] = ids[pl.ds(i * YN * CAP + y * CAP + c, 1), :]
        for start in range(0, BLOCK, chunk):
            blocks = [grads[b, pl.ds(start, chunk), :].astype(F32) for b in range(grads.shape[0])]
            for (i, c), row in rows.items():
                picked = jnp.where(row == 0.0, blocks[0], 0.0)
                for b in range(1, len(blocks)):
                    picked = jnp.where(row == float(b), blocks[b], picked)
                spot = pl.multiple_of((y * CAP + c) * BLOCK + start, chunk)
                (held, o1, o2, o3)[i][pl.ds(spot, chunk), :] = picked.astype(BF16)
    store = pltpu.make_async_copy(held, own, sem)
    store.start()
    store.wait()


def reply_slots(ids, grads, blocks_dev):
    channels = grads[0].shape[1]
    out = jax.ShapeDtypeStruct((YN * CAP * BLOCK, channels), BF16)
    grads = [g.reshape(blocks_dev, BLOCK, channels) for g in grads]
    return kernel_call(
        reply_kernel,
        "slot_replies",
        (out,) * XN,
        [(VMEM, a) for a in (ids, *grads)],
        6,
        REPLY_FLOPS,
        [pltpu.VMEM(out.shape, BF16), pltpu.SemaphoreType.DMA],
        (HBM,) + (VMEM,) * (XN - 1),
    )


def backward_kernel(
    src, slot, cnt, b0, b1, b2, b3, vals, om2, om1, own, op1, op2, acc, ret, in_sem, out_sem
):
    per_x = YN * CAP
    me_x, _ = position()
    load = pltpu.make_async_copy(b0, ret.at[pl.ds(me_x * per_x, per_x)], in_sem)
    load.start()
    for k, back in ((1, b1), (2, b2), (3, b3)):
        x = lax.rem(me_x + k, XN)
        for j in range(per_x):
            ret[x * per_x + j] = back[pl.ds(j * BLOCK, BLOCK), :]
    load.wait()
    steps = cnt.shape[1]
    tiles_step = vals.shape[0] // steps
    acc[...] = jnp.zeros_like(acc)
    for k in range(steps):
        for t in range(tiles_step):
            block = ret[slot[t, k]]
            block = jnp.where(t < cnt[0, k], block, jnp.zeros_like(block))
            acc[k, src[t, k]] += lax.dot_general(
                vals[k * tiles_step + t],
                block,
                (((0,), (0,)), ((), ())),
                preferred_element_type=F32,
            )
    store = pltpu.make_async_copy(acc.at[HALF], own, out_sem)
    store.start()
    for k, out in ((0, om2), (1, om1), (3, op1), (4, op2)):
        for b in range(acc.shape[1]):
            out[pl.ds(b * BLOCK, BLOCK), :] = acc[k, b].astype(BF16)
    store.wait()


def backward_products(src, slot, cnt, back, vals, blocks_dev):
    nodes, channels = blocks_dev * BLOCK, back[0].shape[1]
    steps = cnt.shape[1]
    send = jax.ShapeDtypeStruct((nodes, channels), BF16)
    own = jax.ShapeDtypeStruct((blocks_dev, BLOCK, channels), F32)
    own_back = back[0].reshape(YN * CAP, BLOCK, channels)
    return kernel_call(
        backward_kernel,
        "tile_backward",
        (send, send, own, send, send),
        [(SMEM, a) for a in (src, slot, cnt)]
        + [(HBM, own_back)]
        + [(VMEM, a) for a in (*back[1:], vals)],
        12,
        BACK_FLOPS,
        [
            pltpu.VMEM((steps, blocks_dev, BLOCK, channels), F32),
            pltpu.VMEM((XN * YN * CAP, BLOCK, channels), BF16),
            pltpu.SemaphoreType.DMA,
            pltpu.SemaphoreType.DMA,
        ],
        (VMEM, VMEM, HBM, VMEM, VMEM),
    )


def final_kernel(own, r1, r2, r3, r4, out, held, sem):
    load = pltpu.make_async_copy(own, held, sem)
    load.start()
    load.wait()
    for b in range(held.shape[0]):
        spot = pl.ds(b * BLOCK, BLOCK)
        total = held[b]
        for r in (r1, r2, r3, r4):
            total = total + r[spot, :].astype(F32)
        out[spot, :] = total.astype(BF16)


def final_sum(own, parts):
    return kernel_call(
        final_kernel,
        "grad_sum",
        jax.ShapeDtypeStruct(parts[0].shape, BF16),
        [(HBM, own)] + [(VMEM, a) for a in parts],
        4,
        FINAL_FLOPS,
        [pltpu.VMEM(own.shape, F32), pltpu.SemaphoreType.DMA],
    )


def spread_kernel(parts, out):
    total = parts[0].astype(F32)
    for i in range(1, parts.shape[0]):
        total = total + parts[i].astype(F32)
    for i in range(out.shape[0]):
        out[i] = total.astype(out.dtype)


def sum_and_spread(parts, copies, dtype=F32):
    return kernel_call(
        spread_kernel,
        "sum_and_spread",
        jax.ShapeDtypeStruct((copies,) + parts.shape[1:], dtype),
        [(VMEM, parts)],
        2,
        SPREAD_FLOPS,
    )


def weight_piece(local_grad):
    rows, dom = lax.axis_size("rows"), lax.axis_size("dom")
    outer = dom // INNER
    near = [[i * INNER + j for j in range(INNER)] for i in range(outer)]
    far = [[i * INNER + j for i in range(outer)] for j in range(INNER)]
    pieces = local_grad.reshape(rows, local_grad.shape[0] // rows, local_grad.shape[1])
    piece = sum_and_spread(exchange(pieces, "rows"), INNER)
    piece = sum_and_spread(exchange(piece, "dom", near), outer)
    return sum_and_spread(exchange(piece, "dom", far), rows, BF16)


def per_device(
    features, weight, tile_values, tile_source, tile_slot, slot_block, tile_count, cotangent
):
    blocks_dev = features.shape[0] // BLOCK
    channels = features.shape[1]
    vals = tile_values.reshape(-1, BLOCK, BLOCK)
    src, slot = tile_source[0].T, tile_slot[0].T
    cnt = tile_count

    near = [dom_shift(features, -o) for o in OFFSETS]
    feats = [near[0], near[1], features, near[2], near[3]]
    feats = [f.reshape(blocks_dev, BLOCK, channels) for f in feats]
    sent = forward_products(src, slot, cnt, feats, vals, slot_block)
    got0 = [sent[0]] + [x_shift(sent[k], k) for k in range(1, XN)]
    got1 = [sent[XN]] + [x_shift(sent[XN + k], k) for k in range(1, XN)]
    *sums0, ids = gather_blocks(got0, blocks_dev)
    agg0 = half_sum([sums0[0]] + [y_shift(sums0[k], k) for k in range(1, YN)])
    sums1 = gather_blocks(got1, blocks_dev, ids)
    parts = [sums1[0]] + [y_shift(sums1[k], k) for k in range(1, YN)]
    activations, grad, local_grad = dense(agg0, parts, weight, cotangent)

    piece = weight_piece(local_grad)
    grads = [grad] + [y_shift(grad, k) for k in range(1, YN)]
    reply = reply_slots(ids, grads, blocks_dev)
    back = [reply[0]] + [None] * (XN - 1)
    for k in (1, 3, 2):
        back[k] = x_shift(reply[k], -k)
    terms = list(backward_products(src, slot, cnt, back, vals, blocks_dev))
    own = terms.pop(HALF)
    terms = [dom_shift(t, o) for t, o in zip(terms, OFFSETS)]
    weight_grad = exchange(piece, "rows").reshape(local_grad.shape).astype(F32)
    feature_grad = final_sum(own, terms)
    return (activations, feature_grad, weight_grad)


def solution(mesh):
    return jax.shard_map(
        per_device,
        mesh=mesh,
        in_specs=(
            P(("dom", "rows"), None),
            P(),
            P(("dom", "rows"), None, None, None, None),
            P(("dom", "rows"), None, None),
            P(("dom", "rows"), None, None),
            P(("dom", "rows"), None),
            P(("dom", "rows"), None),
            P(("dom", "rows"), None),
        ),
        out_specs=(P(("dom", "rows"), None), P(("dom", "rows"), None), P()),
        check_vma=False,
    )
```

```python
import functools

import jax
import jax.numpy as jnp
from jax import lax
from jax.experimental import pallas as pl
from jax.experimental.pallas import tpu as pltpu
from jax.sharding import PartitionSpec as P

BLOCK = 128
HALF = 2
CAP = 2
XN = 4
YN = 4
INNER = 8
LANES = 128
ID_ROWS = 16
FORWARD_MIB = 56

OFFSETS = (-2, -1, 1, 2)
VMEM = pl.BlockSpec(memory_space=pltpu.VMEM)
HBM = pl.BlockSpec(memory_space=pltpu.HBM)
SMEM = pl.BlockSpec(memory_space=pltpu.SMEM)
BF16 = jnp.bfloat16
F32 = jnp.float32

GATHER_FLOPS = 10**11
HALF_FLOPS = 10**10
DENSE_FLOPS = 1 << 28
REPLY_FLOPS = 10**10
BACK_FLOPS = 10**10
FINAL_FLOPS = 10**10
SPREAD_FLOPS = 1 << 16


def kernel_call(body, name, outs, ins, mib, flops, scratch=(), out_specs=None):
    nbytes = sum(a.size * a.dtype.itemsize for _, a in ins)
    return pl.pallas_call(
        body,
        out_shape=outs,
        in_specs=[space for space, _ in ins],
        out_specs=out_specs or jax.tree.map(lambda _: VMEM, outs),
        scratch_shapes=list(scratch),
        compiler_params=pltpu.CompilerParams(vmem_limit_bytes=mib << 20),
        cost_estimate=pl.CostEstimate(flops=flops, bytes_accessed=nbytes, transcendentals=0),
        name=name,
    )(*[a for _, a in ins])


def dom_shift(value, steps):
    count = lax.axis_size("dom")
    return lax.ppermute(value, "dom", [(i, (i + steps) % count) for i in range(count)])


def y_shift(value, steps):
    pairs = [(x * YN + y, x * YN + (y + steps) % YN) for x in range(XN) for y in range(YN)]
    return lax.ppermute(value, "rows", pairs)


def x_shift(value, steps):
    pairs = [(x * YN + y, (x + steps) % XN * YN + y) for x in range(XN) for y in range(YN)]
    return lax.ppermute(value, "rows", pairs)


X_GROUPS = [[x * YN + y for x in range(XN)] for y in range(YN)]
Y_GROUPS = [[x * YN + y for y in range(YN)] for x in range(XN)]


def exchange(value, axis, groups=None):
    return lax.all_to_all(
        value, axis, split_axis=0, concat_axis=0, tiled=True, axis_index_groups=groups
    )


def position():
    rank = lax.axis_index("rows")
    return lax.div(rank, YN), lax.rem(rank, YN)


def forward_kernel(src, slot, cnt, ids, fm2, fm1, f0, fp1, fp2, vals, *refs):
    outs, acc = refs[:-1], refs[-1]
    acc[...] = jnp.zeros_like(acc)
    feats = (fm2, fm1, f0, fp1, fp2)
    tiles_step = vals.shape[0] // len(feats)
    for k, feat in enumerate(feats):
        for t in range(tiles_step):
            block = feat[src[t, k]]
            block = jnp.where(t < cnt[0, k], block, jnp.zeros_like(block))
            acc[slot[t, k]] += jnp.dot(
                vals[k * tiles_step + t], block, preferred_element_type=F32
            )
    me_x, _ = position()
    per_x = YN * CAP
    line = lax.broadcasted_iota(jnp.int32, (ID_ROWS, LANES), 0)
    for k in range(XN):
        x = lax.rem(me_x + k, XN)
        rows = jnp.zeros_like(line)
        for j in range(per_x):
            total = acc[x * per_x + j].astype(BF16)
            rows = jnp.where(line == j, ids[0, x * per_x + j], rows)
            for h in range(2):
                part = total[:, h * LANES : (h + 1) * LANES]
                outs[h * XN + k][pl.ds(j * BLOCK, BLOCK), :] = part
        outs[k][pl.ds(per_x * BLOCK, ID_ROWS), :] = rows.astype(F32).astype(BF16)


def forward_products(src, slot, cnt, feats, vals, ids):
    rows = YN * CAP * BLOCK
    first = jax.ShapeDtypeStruct((rows + ID_ROWS, LANES), BF16)
    second = jax.ShapeDtypeStruct((rows, LANES), BF16)
    return kernel_call(
        forward_kernel,
        "tile_forward",
        (first,) * XN + (second,) * XN,
        [(SMEM, a) for a in (src, slot, cnt, ids)] + [(VMEM, a) for a in (*feats, vals)],
        FORWARD_MIB,
        vals.size * 4 * LANES,
        [pltpu.VMEM((XN * YN * CAP, BLOCK, 2 * LANES), F32)],
    )


def gather_kernel(blocks_dev, recv, ids, outs):
    _, me_y = position()
    chunk = 64
    for i, out in enumerate(outs):
        y = lax.rem(me_y + i, YN)
        rows = {}
        for k in range(XN):
            for c in range(CAP):
                rows[k, c] = ids[pl.ds(k * YN * CAP + y * CAP + c, 1), :][:, :LANES]
        for start in range(0, BLOCK, chunk):
            totals = [jnp.zeros((chunk, LANES), F32) for _ in range(blocks_dev)]
            for (k, c), row in rows.items():
                spot = pl.multiple_of((y * CAP + c) * BLOCK + start, chunk)
                part = recv[k][pl.ds(spot, chunk), :].astype(F32)
                for b in range(blocks_dev):
                    totals[b] = totals[b] + jnp.where(row == float(b), part, 0.0)
            for b in range(blocks_dev):
                out[pl.ds(b * BLOCK + start, chunk), :] = totals[b].astype(BF16)


def gather0_kernel(blocks_dev, *refs):
    recv, outs, ids = refs[:XN], refs[XN:-1], refs[-1]
    per_x = YN * CAP
    for k in range(XN):
        got = recv[k][pl.ds(per_x * BLOCK, ID_ROWS), :].astype(F32)[:per_x]
        ids[pl.ds(k * per_x, per_x), :] = jnp.concatenate([got, got], axis=1)
    gather_kernel(blocks_dev, recv, ids, outs)


def gather1_kernel(blocks_dev, *refs):
    gather_kernel(blocks_dev, refs[:XN], refs[XN], refs[XN + 1 :])


def gather_blocks(recv, blocks_dev, ids=None):
    outs = (jax.ShapeDtypeStruct((blocks_dev * BLOCK, LANES), BF16),) * YN
    if ids is None:
        outs += (jax.ShapeDtypeStruct((XN * YN * CAP, 2 * LANES), F32),)
    return kernel_call(
        functools.partial(gather0_kernel if ids is None else gather1_kernel, blocks_dev),
        "block_sums",
        outs,
        [(VMEM, a) for a in recv] + ([] if ids is None else [(VMEM, ids)]),
        6,
        GATHER_FLOPS,
    )


def summed(parts):
    total = parts[0][...].astype(F32)
    for part in parts[1:]:
        total = total + part[...].astype(F32)
    return total.astype(BF16)


def half_kernel(*refs):
    refs[-1][...] = summed(refs[:-1])


def half_sum(parts):
    return kernel_call(
        half_kernel,
        "half_sum",
        jax.ShapeDtypeStruct(parts[0].shape, BF16),
        [(VMEM, a) for a in parts],
        4,
        HALF_FLOPS,
    )


def dense_kernel(*refs):
    agg0, parts, (weight, cot, act, grad, wgrad) = refs[0], refs[1 : 1 + YN], refs[1 + YN :]
    agg = jnp.concatenate([agg0[...], summed(parts)], axis=1)
    w = weight[...]
    pre = jnp.dot(agg, w, preferred_element_type=F32)
    sig = 1.0 / (1.0 + jnp.exp(-pre))
    act[...] = (pre * sig).astype(BF16)
    slope = sig * (1.0 + pre * (1.0 - sig))
    pre_grad = (cot[...].astype(F32) * slope).astype(BF16)
    grad[...] = lax.dot_general(
        pre_grad, w, (((1,), (1,)), ((), ())), preferred_element_type=F32
    ).astype(BF16)
    wgrad[...] = lax.dot_general(
        agg, pre_grad, (((0,), (0,)), ((), ())), preferred_element_type=F32
    ).astype(BF16)


def dense(agg0, parts, weight, cot):
    nodes, channels = cot.shape
    full = jax.ShapeDtypeStruct((nodes, channels), BF16)
    return kernel_call(
        dense_kernel,
        "dense_layer",
        (full, full, jax.ShapeDtypeStruct((channels, channels), BF16)),
        [(VMEM, a) for a in (agg0, *parts, weight, cot)],
        10,
        DENSE_FLOPS,
    )


def reply_kernel(ids, g0, r1, r2, r3, own, o1, o2, o3, held, sem):
    _, me_y = position()
    chunk = 32
    for k, grads in enumerate((g0, r1, r2, r3)):
        y = lax.rem(me_y - k + YN, YN)
        rows = {}
        for i in range(XN):
            for c in range(CAP):
                rows[i, c] = ids[pl.ds(i * YN * CAP + y * CAP + c, 1), :]
        for start in range(0, BLOCK, chunk):
            blocks = [grads[b, pl.ds(start, chunk), :].astype(F32) for b in range(grads.shape[0])]
            for (i, c), row in rows.items():
                picked = jnp.where(row == 0.0, blocks[0], 0.0)
                for b in range(1, len(blocks)):
                    picked = jnp.where(row == float(b), blocks[b], picked)
                spot = pl.multiple_of((y * CAP + c) * BLOCK + start, chunk)
                (held, o1, o2, o3)[i][pl.ds(spot, chunk), :] = picked.astype(BF16)
    store = pltpu.make_async_copy(held, own, sem)
    store.start()
    store.wait()


def reply_slots(ids, grads, blocks_dev):
    channels = grads[0].shape[1]
    out = jax.ShapeDtypeStruct((YN * CAP * BLOCK, channels), BF16)
    grads = [g.reshape(blocks_dev, BLOCK, channels) for g in grads]
    return kernel_call(
        reply_kernel,
        "slot_replies",
        (out,) * XN,
        [(VMEM, a) for a in (ids, *grads)],
        6,
        REPLY_FLOPS,
        [pltpu.VMEM(out.shape, BF16), pltpu.SemaphoreType.DMA],
        (HBM,) + (VMEM,) * (XN - 1),
    )


def backward_kernel(
    src, slot, cnt, b0, b1, b2, b3, vals, om2, om1, own, op1, op2, acc, ret, in_sem, out_sem
):
    per_x = YN * CAP
    me_x, _ = position()
    load = pltpu.make_async_copy(b0, ret.at[pl.ds(me_x * per_x, per_x)], in_sem)
    load.start()
    for k, back in ((1, b1), (2, b2), (3, b3)):
        x = lax.rem(me_x + k, XN)
        for j in range(per_x):
            ret[x * per_x + j] = back[pl.ds(j * BLOCK, BLOCK), :]
    load.wait()
    steps = cnt.shape[1]
    tiles_step = vals.shape[0] // steps
    acc[...] = jnp.zeros_like(acc)
    for k in range(steps):
        for t in range(tiles_step):
            block = ret[slot[t, k]]
            block = jnp.where(t < cnt[0, k], block, jnp.zeros_like(block))
            acc[k, src[t, k]] += lax.dot_general(
                vals[k * tiles_step + t],
                block,
                (((0,), (0,)), ((), ())),
                preferred_element_type=F32,
            )
    store = pltpu.make_async_copy(acc.at[HALF], own, out_sem)
    store.start()
    for k, out in ((0, om2), (1, om1), (3, op1), (4, op2)):
        for b in range(acc.shape[1]):
            out[pl.ds(b * BLOCK, BLOCK), :] = acc[k, b].astype(BF16)
    store.wait()


def backward_products(src, slot, cnt, back, vals, blocks_dev):
    nodes, channels = blocks_dev * BLOCK, back[0].shape[1]
    steps = cnt.shape[1]
    send = jax.ShapeDtypeStruct((nodes, channels), BF16)
    own = jax.ShapeDtypeStruct((blocks_dev, BLOCK, channels), F32)
    own_back = back[0].reshape(YN * CAP, BLOCK, channels)
    return kernel_call(
        backward_kernel,
        "tile_backward",
        (send, send, own, send, send),
        [(SMEM, a) for a in (src, slot, cnt)]
        + [(HBM, own_back)]
        + [(VMEM, a) for a in (*back[1:], vals)],
        12,
        BACK_FLOPS,
        [
            pltpu.VMEM((steps, blocks_dev, BLOCK, channels), F32),
            pltpu.VMEM((XN * YN * CAP, BLOCK, channels), BF16),
            pltpu.SemaphoreType.DMA,
            pltpu.SemaphoreType.DMA,
        ],
        (VMEM, VMEM, HBM, VMEM, VMEM),
    )


def final_kernel(own, r1, r2, r3, r4, out, held, sem):
    load = pltpu.make_async_copy(own, held, sem)
    load.start()
    load.wait()
    for b in range(held.shape[0]):
        spot = pl.ds(b * BLOCK, BLOCK)
        total = held[b]
        for r in (r1, r2, r3, r4):
            total = total + r[spot, :].astype(F32)
        out[spot, :] = total.astype(BF16)


def final_sum(own, parts):
    return kernel_call(
        final_kernel,
        "grad_sum",
        jax.ShapeDtypeStruct(parts[0].shape, BF16),
        [(HBM, own)] + [(VMEM, a) for a in parts],
        4,
        FINAL_FLOPS,
        [pltpu.VMEM(own.shape, F32), pltpu.SemaphoreType.DMA],
    )


def spread_kernel(parts, out):
    total = parts[0].astype(F32)
    for i in range(1, parts.shape[0]):
        total = total + parts[i].astype(F32)
    for i in range(out.shape[0]):
        out[i] = total.astype(out.dtype)


def sum_and_spread(parts, copies, dtype=F32):
    return kernel_call(
        spread_kernel,
        "sum_and_spread",
        jax.ShapeDtypeStruct((copies,) + parts.shape[1:], dtype),
        [(VMEM, parts)],
        2,
        SPREAD_FLOPS,
    )


def weight_piece(local_grad):
    rows, dom = lax.axis_size("rows"), lax.axis_size("dom")
    outer = dom // INNER
    near = [[i * INNER + j for j in range(INNER)] for i in range(outer)]
    far = [[i * INNER + j for i in range(outer)] for j in range(INNER)]
    pieces = local_grad.reshape(rows, local_grad.shape[0] // rows, local_grad.shape[1])
    piece = sum_and_spread(exchange(pieces, "rows"), INNER)
    piece = sum_and_spread(exchange(piece, "dom", near), outer)
    return sum_and_spread(exchange(piece, "dom", far), XN, BF16)


def per_device(
    features, weight, tile_values, tile_source, tile_slot, slot_block, tile_count, cotangent
):
    blocks_dev = features.shape[0] // BLOCK
    channels = features.shape[1]
    vals = tile_values.reshape(-1, BLOCK, BLOCK)
    src, slot = tile_source[0].T, tile_slot[0].T
    cnt = tile_count

    near = [dom_shift(features, -o) for o in OFFSETS]
    feats = [near[0], near[1], features, near[2], near[3]]
    feats = [f.reshape(blocks_dev, BLOCK, channels) for f in feats]
    sent = forward_products(src, slot, cnt, feats, vals, slot_block)
    got0, got1 = list(sent[:XN]), list(sent[XN:])
    for got in (got0, got1):
        for k in (1, 3, 2):
            got[k] = x_shift(got[k], k)
    *sums0, ids = gather_blocks(got0, blocks_dev)
    agg0 = half_sum([sums0[0]] + [y_shift(sums0[k], k) for k in range(1, YN)])
    sums1 = gather_blocks(got1, blocks_dev, ids)
    parts = [sums1[0]] + [y_shift(sums1[k], k) for k in range(1, YN)]
    activations, grad, local_grad = dense(agg0, parts, weight, cotangent)

    piece = weight_piece(local_grad)
    grads = [grad] + [y_shift(grad, k) for k in range(1, YN)]
    reply = reply_slots(ids, grads, blocks_dev)
    back = [reply[0]] + [None] * (XN - 1)
    for k in (1, 3, 2):
        back[k] = x_shift(reply[k], -k)
    terms = list(backward_products(src, slot, cnt, back, vals, blocks_dev))
    own = terms.pop(HALF)
    terms = [dom_shift(t, o) for t, o in zip(terms, OFFSETS)]
    column = exchange(piece, "rows", X_GROUPS)
    column = jnp.broadcast_to(column.reshape(1, -1, channels), (YN, channels // YN, channels))
    whole = exchange(column, "rows", Y_GROUPS).reshape(YN, XN, -1, channels)
    weight_grad = whole.transpose(1, 0, 2, 3).reshape(local_grad.shape).astype(F32)
    feature_grad = final_sum(own, terms)
    return (activations, feature_grad, weight_grad)


def solution(mesh):
    return jax.shard_map(
        per_device,
        mesh=mesh,
        in_specs=(
            P(("dom", "rows"), None),
            P(),
            P(("dom", "rows"), None, None, None, None),
            P(("dom", "rows"), None, None),
            P(("dom", "rows"), None, None),
            P(("dom", "rows"), None),
            P(("dom", "rows"), None),
            P(("dom", "rows"), None),
        ),
        out_specs=(P(("dom", "rows"), None), P(("dom", "rows"), None), P()),
        check_vma=False,
    )
```

```python
import functools

import jax
import jax.numpy as jnp
from jax import lax
from jax.experimental import pallas as pl
from jax.experimental.pallas import tpu as pltpu
from jax.sharding import PartitionSpec as P

BLOCK = 128
HALF = 2
CAP = 2
XN = 4
YN = 4
INNER = 8
LANES = 128
ID_ROWS = 16
FORWARD_MIB = 56

OFFSETS = (-2, -1, 1, 2)
VMEM = pl.BlockSpec(memory_space=pltpu.VMEM)
HBM = pl.BlockSpec(memory_space=pltpu.HBM)
SMEM = pl.BlockSpec(memory_space=pltpu.SMEM)
BF16 = jnp.bfloat16
F32 = jnp.float32

GATHER_FLOPS = 10**11
HALF_FLOPS = 10**10
DENSE_FLOPS = 1 << 28
REPLY_FLOPS = 10**10
BACK_FLOPS = 10**10
FINAL_FLOPS = 10**10
SPREAD_FLOPS = 1 << 16


def kernel_call(body, name, outs, ins, mib, flops, scratch=(), out_specs=None):
    nbytes = sum(a.size * a.dtype.itemsize for _, a in ins)
    return pl.pallas_call(
        body,
        out_shape=outs,
        in_specs=[space for space, _ in ins],
        out_specs=out_specs or jax.tree.map(lambda _: VMEM, outs),
        scratch_shapes=list(scratch),
        compiler_params=pltpu.CompilerParams(vmem_limit_bytes=mib << 20),
        cost_estimate=pl.CostEstimate(flops=flops, bytes_accessed=nbytes, transcendentals=0),
        name=name,
    )(*[a for _, a in ins])


def dom_shift(value, steps):
    count = lax.axis_size("dom")
    return lax.ppermute(value, "dom", [(i, (i + steps) % count) for i in range(count)])


def y_shift(value, steps):
    pairs = [(x * YN + y, x * YN + (y + steps) % YN) for x in range(XN) for y in range(YN)]
    return lax.ppermute(value, "rows", pairs)


def x_shift(value, steps):
    pairs = [(x * YN + y, (x + steps) % XN * YN + y) for x in range(XN) for y in range(YN)]
    return lax.ppermute(value, "rows", pairs)


X_GROUPS = [[x * YN + y for x in range(XN)] for y in range(YN)]
Y_GROUPS = [[x * YN + y for y in range(YN)] for x in range(XN)]


def exchange(value, axis, groups=None):
    return lax.all_to_all(
        value, axis, split_axis=0, concat_axis=0, tiled=True, axis_index_groups=groups
    )


def position():
    rank = lax.axis_index("rows")
    return lax.div(rank, YN), lax.rem(rank, YN)


def forward_kernel(src, slot, cnt, ids, fm2, fm1, f0, fp1, fp2, vals, *refs):
    outs, acc = refs[:-1], refs[-1]
    acc[...] = jnp.zeros_like(acc)
    feats = (fm2, fm1, f0, fp1, fp2)
    tiles_step = vals.shape[0] // len(feats)
    for k, feat in enumerate(feats):
        for t in range(tiles_step):
            block = feat[src[t, k]]
            block = jnp.where(t < cnt[0, k], block, jnp.zeros_like(block))
            acc[slot[t, k]] += jnp.dot(
                vals[k * tiles_step + t], block, preferred_element_type=F32
            )
    me_x, _ = position()
    per_x = YN * CAP
    line = lax.broadcasted_iota(jnp.int32, (ID_ROWS, LANES), 0)
    for k in range(XN):
        x = lax.rem(me_x + k, XN)
        rows = jnp.zeros_like(line)
        for j in range(per_x):
            total = acc[x * per_x + j].astype(BF16)
            rows = jnp.where(line == j, ids[0, x * per_x + j], rows)
            for h in range(2):
                part = total[:, h * LANES : (h + 1) * LANES]
                outs[h * XN + k][pl.ds(j * BLOCK, BLOCK), :] = part
        outs[k][pl.ds(per_x * BLOCK, ID_ROWS), :] = rows.astype(F32).astype(BF16)


def forward_products(src, slot, cnt, feats, vals, ids):
    rows = YN * CAP * BLOCK
    first = jax.ShapeDtypeStruct((rows + ID_ROWS, LANES), BF16)
    second = jax.ShapeDtypeStruct((rows, LANES), BF16)
    return kernel_call(
        forward_kernel,
        "tile_forward",
        (first,) * XN + (second,) * XN,
        [(SMEM, a) for a in (src, slot, cnt, ids)] + [(VMEM, a) for a in (*feats, vals)],
        FORWARD_MIB,
        vals.size * 4 * LANES,
        [pltpu.VMEM((XN * YN * CAP, BLOCK, 2 * LANES), F32)],
    )


def gather_kernel(blocks_dev, recv, ids, outs):
    _, me_y = position()
    chunk = 64
    for i, out in enumerate(outs):
        y = lax.rem(me_y + i, YN)
        rows = {}
        for k in range(XN):
            for c in range(CAP):
                rows[k, c] = ids[pl.ds(k * YN * CAP + y * CAP + c, 1), :][:, :LANES]
        for start in range(0, BLOCK, chunk):
            totals = [jnp.zeros((chunk, LANES), F32) for _ in range(blocks_dev)]
            for (k, c), row in rows.items():
                spot = pl.multiple_of((y * CAP + c) * BLOCK + start, chunk)
                part = recv[k][pl.ds(spot, chunk), :].astype(F32)
                for b in range(blocks_dev):
                    totals[b] = totals[b] + jnp.where(row == float(b), part, 0.0)
            for b in range(blocks_dev):
                out[pl.ds(b * BLOCK + start, chunk), :] = totals[b].astype(BF16)


def gather0_kernel(blocks_dev, *refs):
    recv, outs, ids = refs[:XN], refs[XN:-1], refs[-1]
    per_x = YN * CAP
    for k in range(XN):
        got = recv[k][pl.ds(per_x * BLOCK, ID_ROWS), :].astype(F32)[:per_x]
        ids[pl.ds(k * per_x, per_x), :] = jnp.concatenate([got, got], axis=1)
    gather_kernel(blocks_dev, recv, ids, outs)


def gather1_kernel(blocks_dev, *refs):
    recv, ids, first = refs[:XN], refs[XN], refs[XN + 1]
    own, o1, o2, o3 = refs[XN + 2 :]
    nodes = blocks_dev * BLOCK
    o2[pl.ds(0, nodes), :] = first[...]
    gather_kernel(blocks_dev, recv, ids, (own, o1, o2.at[pl.ds(nodes, nodes)], o3))


def gather_blocks(recv, blocks_dev, ids=None, first=None):
    half = jax.ShapeDtypeStruct((blocks_dev * BLOCK, LANES), BF16)
    if ids is None:
        outs = (half,) * YN + (jax.ShapeDtypeStruct((XN * YN * CAP, 2 * LANES), F32),)
    else:
        outs = (half, half, jax.ShapeDtypeStruct((2 * blocks_dev * BLOCK, LANES), BF16), half)
    return kernel_call(
        functools.partial(gather0_kernel if ids is None else gather1_kernel, blocks_dev),
        "block_sums",
        outs,
        [(VMEM, a) for a in recv] + ([] if ids is None else [(VMEM, ids), (VMEM, first)]),
        6,
        GATHER_FLOPS,
    )


def summed(parts):
    total = parts[0][...].astype(F32)
    for part in parts[1:]:
        total = total + part[...].astype(F32)
    return total


def half_kernel(*refs):
    refs[-1][...] = summed(refs[:-1])


def half_sum(parts):
    return kernel_call(
        half_kernel,
        "half_sum",
        jax.ShapeDtypeStruct(parts[0].shape, F32),
        [(VMEM, a) for a in parts],
        4,
        HALF_FLOPS,
    )


def dense_kernel(*refs):
    sum0, both, parts = refs[0], refs[1], refs[2 : 1 + YN]
    weight, cot, act, grad, wgrad = refs[1 + YN :]
    nodes = cot.shape[0]
    left = sum0[...] + both[pl.ds(0, nodes), :].astype(F32)
    right = summed(parts) + both[pl.ds(nodes, nodes), :].astype(F32)
    agg = jnp.concatenate([left, right], axis=1).astype(BF16)
    w = weight[...]
    pre = jnp.dot(agg, w, preferred_element_type=F32)
    sig = 1.0 / (1.0 + jnp.exp(-pre))
    act[...] = (pre * sig).astype(BF16)
    slope = sig * (1.0 + pre * (1.0 - sig))
    pre_grad = (cot[...].astype(F32) * slope).astype(BF16)
    grad[...] = lax.dot_general(
        pre_grad, w, (((1,), (1,)), ((), ())), preferred_element_type=F32
    ).astype(BF16)
    wgrad[...] = lax.dot_general(
        agg, pre_grad, (((0,), (0,)), ((), ())), preferred_element_type=F32
    ).astype(BF16)


def dense(sum0, both, parts, weight, cot):
    nodes, channels = cot.shape
    full = jax.ShapeDtypeStruct((nodes, channels), BF16)
    return kernel_call(
        dense_kernel,
        "dense_layer",
        (full, full, jax.ShapeDtypeStruct((channels, channels), BF16)),
        [(VMEM, a) for a in (sum0, both, *parts, weight, cot)],
        10,
        DENSE_FLOPS,
    )


def reply_kernel(ids, g0, r1, r2, r3, own, o1, o2, o3, held, sem):
    _, me_y = position()
    chunk = 32
    for k, grads in enumerate((g0, r1, r2, r3)):
        y = lax.rem(me_y - k + YN, YN)
        rows = {}
        for i in range(XN):
            for c in range(CAP):
                rows[i, c] = ids[pl.ds(i * YN * CAP + y * CAP + c, 1), :]
        for start in range(0, BLOCK, chunk):
            blocks = [grads[b, pl.ds(start, chunk), :].astype(F32) for b in range(grads.shape[0])]
            for (i, c), row in rows.items():
                picked = jnp.where(row == 0.0, blocks[0], 0.0)
                for b in range(1, len(blocks)):
                    picked = jnp.where(row == float(b), blocks[b], picked)
                spot = pl.multiple_of((y * CAP + c) * BLOCK + start, chunk)
                (held, o1, o2, o3)[i][pl.ds(spot, chunk), :] = picked.astype(BF16)
    store = pltpu.make_async_copy(held, own, sem)
    store.start()
    store.wait()


def reply_slots(ids, grads, blocks_dev):
    channels = grads[0].shape[1]
    out = jax.ShapeDtypeStruct((YN * CAP * BLOCK, channels), BF16)
    grads = [g.reshape(blocks_dev, BLOCK, channels) for g in grads]
    return kernel_call(
        reply_kernel,
        "slot_replies",
        (out,) * XN,
        [(VMEM, a) for a in (ids, *grads)],
        6,
        REPLY_FLOPS,
        [pltpu.VMEM(out.shape, BF16), pltpu.SemaphoreType.DMA],
        (HBM,) + (VMEM,) * (XN - 1),
    )


def backward_kernel(
    src, slot, cnt, b0, b1, b2, b3, vals, om2, om1, own, op1, op2, acc, ret, in_sem, out_sem
):
    per_x = YN * CAP
    me_x, _ = position()
    load = pltpu.make_async_copy(b0, ret.at[pl.ds(me_x * per_x, per_x)], in_sem)
    load.start()
    for k, back in ((1, b1), (2, b2), (3, b3)):
        x = lax.rem(me_x + k, XN)
        for j in range(per_x):
            ret[x * per_x + j] = back[pl.ds(j * BLOCK, BLOCK), :]
    load.wait()
    steps = cnt.shape[1]
    tiles_step = vals.shape[0] // steps
    acc[...] = jnp.zeros_like(acc)
    for k in range(steps):
        for t in range(tiles_step):
            block = ret[slot[t, k]]
            block = jnp.where(t < cnt[0, k], block, jnp.zeros_like(block))
            acc[k, src[t, k]] += lax.dot_general(
                vals[k * tiles_step + t],
                block,
                (((0,), (0,)), ((), ())),
                preferred_element_type=F32,
            )
    store = pltpu.make_async_copy(acc.at[HALF], own, out_sem)
    store.start()
    for k, out in ((0, om2), (1, om1), (3, op1), (4, op2)):
        for b in range(acc.shape[1]):
            out[pl.ds(b * BLOCK, BLOCK), :] = acc[k, b].astype(BF16)
    store.wait()


def backward_products(src, slot, cnt, back, vals, blocks_dev):
    nodes, channels = blocks_dev * BLOCK, back[0].shape[1]
    steps = cnt.shape[1]
    send = jax.ShapeDtypeStruct((nodes, channels), BF16)
    own = jax.ShapeDtypeStruct((blocks_dev, BLOCK, channels), F32)
    own_back = back[0].reshape(YN * CAP, BLOCK, channels)
    return kernel_call(
        backward_kernel,
        "tile_backward",
        (send, send, own, send, send),
        [(SMEM, a) for a in (src, slot, cnt)]
        + [(HBM, own_back)]
        + [(VMEM, a) for a in (*back[1:], vals)],
        12,
        BACK_FLOPS,
        [
            pltpu.VMEM((steps, blocks_dev, BLOCK, channels), F32),
            pltpu.VMEM((XN * YN * CAP, BLOCK, channels), BF16),
            pltpu.SemaphoreType.DMA,
            pltpu.SemaphoreType.DMA,
        ],
        (VMEM, VMEM, HBM, VMEM, VMEM),
    )


def final_kernel(own, r1, r2, r3, r4, out, held, sem):
    load = pltpu.make_async_copy(own, held, sem)
    load.start()
    load.wait()
    for b in range(held.shape[0]):
        spot = pl.ds(b * BLOCK, BLOCK)
        total = held[b]
        for r in (r1, r2, r3, r4):
            total = total + r[spot, :].astype(F32)
        out[spot, :] = total.astype(BF16)


def final_sum(own, parts):
    return kernel_call(
        final_kernel,
        "grad_sum",
        jax.ShapeDtypeStruct(parts[0].shape, BF16),
        [(HBM, own)] + [(VMEM, a) for a in parts],
        4,
        FINAL_FLOPS,
        [pltpu.VMEM(own.shape, F32), pltpu.SemaphoreType.DMA],
    )


def spread_kernel(parts, out):
    total = parts[0].astype(F32)
    for i in range(1, parts.shape[0]):
        total = total + parts[i].astype(F32)
    for i in range(out.shape[0]):
        out[i] = total.astype(out.dtype)


def sum_and_spread(parts, copies, dtype=F32):
    return kernel_call(
        spread_kernel,
        "sum_and_spread",
        jax.ShapeDtypeStruct((copies,) + parts.shape[1:], dtype),
        [(VMEM, parts)],
        2,
        SPREAD_FLOPS,
    )


def weight_piece(local_grad):
    rows, dom = lax.axis_size("rows"), lax.axis_size("dom")
    outer = dom // INNER
    near = [[i * INNER + j for j in range(INNER)] for i in range(outer)]
    far = [[i * INNER + j for i in range(outer)] for j in range(INNER)]
    pieces = local_grad.reshape(rows, local_grad.shape[0] // rows, local_grad.shape[1])
    piece = sum_and_spread(exchange(pieces, "rows"), INNER)
    piece = sum_and_spread(exchange(piece, "dom", near), outer)
    return sum_and_spread(exchange(piece, "dom", far), rows, BF16)


def per_device(
    features, weight, tile_values, tile_source, tile_slot, slot_block, tile_count, cotangent
):
    blocks_dev = features.shape[0] // BLOCK
    channels = features.shape[1]
    vals = tile_values.reshape(-1, BLOCK, BLOCK)
    src, slot = tile_source[0].T, tile_slot[0].T
    cnt = tile_count

    near = [dom_shift(features, -o) for o in OFFSETS]
    feats = [near[0], near[1], features, near[2], near[3]]
    feats = [f.reshape(blocks_dev, BLOCK, channels) for f in feats]
    sent = forward_products(src, slot, cnt, feats, vals, slot_block)
    got0 = [sent[0]] + [x_shift(sent[k], k) for k in range(1, XN)]
    got1 = [sent[XN]] + [x_shift(sent[XN + k], k) for k in range(1, XN)]
    *sums0, ids = gather_blocks(got0, blocks_dev)
    sum0 = half_sum([sums0[0], y_shift(sums0[1], 1), y_shift(sums0[3], 3)])
    sums1 = gather_blocks(got1, blocks_dev, ids, sums0[2])
    both = y_shift(sums1[2], 2)
    parts = [sums1[0], y_shift(sums1[1], 1), y_shift(sums1[3], 3)]
    activations, grad, local_grad = dense(sum0, both, parts, weight, cotangent)

    piece = weight_piece(local_grad)
    grads = [grad] + [y_shift(grad, k) for k in range(1, YN)]
    reply = reply_slots(ids, grads, blocks_dev)
    back = [reply[0]] + [None] * (XN - 1)
    for k in (1, 3, 2):
        back[k] = x_shift(reply[k], -k)
    terms = list(backward_products(src, slot, cnt, back, vals, blocks_dev))
    own = terms.pop(HALF)
    terms = [dom_shift(t, o) for t, o in zip(terms, OFFSETS)]
    weight_grad = exchange(piece, "rows").reshape(local_grad.shape).astype(F32)
    feature_grad = final_sum(own, terms)
    return (activations, feature_grad, weight_grad)


def solution(mesh):
    return jax.shard_map(
        per_device,
        mesh=mesh,
        in_specs=(
            P(("dom", "rows"), None),
            P(),
            P(("dom", "rows"), None, None, None, None),
            P(("dom", "rows"), None, None),
            P(("dom", "rows"), None, None),
            P(("dom", "rows"), None),
            P(("dom", "rows"), None),
            P(("dom", "rows"), None),
        ),
        out_specs=(P(("dom", "rows"), None), P(("dom", "rows"), None), P()),
        check_vma=False,
    )
```

```python
import functools

import jax
import jax.numpy as jnp
from jax import lax
from jax.experimental import pallas as pl
from jax.experimental.pallas import tpu as pltpu
from jax.sharding import PartitionSpec as P

BLOCK = 128
HALF = 2
CAP = 2
XN = 4
YN = 4
INNER = 8
LANES = 128
ID_ROWS = 16
FORWARD_MIB = 56

OFFSETS = (-2, -1, 1, 2)
VMEM = pl.BlockSpec(memory_space=pltpu.VMEM)
HBM = pl.BlockSpec(memory_space=pltpu.HBM)
SMEM = pl.BlockSpec(memory_space=pltpu.SMEM)
BF16 = jnp.bfloat16
F32 = jnp.float32

GATHER_FLOPS = 10**11
HALF_FLOPS = 10**10
DENSE_FLOPS = 1 << 28
REPLY_FLOPS = 10**10
BACK_FLOPS = 10**10
FINAL_FLOPS = 10**10
SPREAD_FLOPS = 1 << 16


def kernel_call(body, name, outs, ins, mib, flops, scratch=(), out_specs=None):
    nbytes = sum(a.size * a.dtype.itemsize for _, a in ins)
    return pl.pallas_call(
        body,
        out_shape=outs,
        in_specs=[space for space, _ in ins],
        out_specs=out_specs or jax.tree.map(lambda _: VMEM, outs),
        scratch_shapes=list(scratch),
        compiler_params=pltpu.CompilerParams(vmem_limit_bytes=mib << 20),
        cost_estimate=pl.CostEstimate(flops=flops, bytes_accessed=nbytes, transcendentals=0),
        name=name,
    )(*[a for _, a in ins])


def dom_shift(value, steps):
    count = lax.axis_size("dom")
    return lax.ppermute(value, "dom", [(i, (i + steps) % count) for i in range(count)])


def y_shift(value, steps):
    pairs = [(x * YN + y, x * YN + (y + steps) % YN) for x in range(XN) for y in range(YN)]
    return lax.ppermute(value, "rows", pairs)


def x_shift(value, steps):
    pairs = [(x * YN + y, (x + steps) % XN * YN + y) for x in range(XN) for y in range(YN)]
    return lax.ppermute(value, "rows", pairs)


X_GROUPS = [[x * YN + y for x in range(XN)] for y in range(YN)]
Y_GROUPS = [[x * YN + y for y in range(YN)] for x in range(XN)]


def exchange(value, axis, groups=None):
    return lax.all_to_all(
        value, axis, split_axis=0, concat_axis=0, tiled=True, axis_index_groups=groups
    )


def position():
    rank = lax.axis_index("rows")
    return lax.div(rank, YN), lax.rem(rank, YN)


def forward_kernel(src, slot, cnt, ids, fm2, fm1, f0, fp1, fp2, vals, *refs):
    outs, acc = refs[:-1], refs[-1]
    acc[...] = jnp.zeros_like(acc)
    feats = (fm2, fm1, f0, fp1, fp2)
    tiles_step = vals.shape[0] // len(feats)
    for k, feat in enumerate(feats):
        for t in range(tiles_step):
            block = feat[src[t, k]]
            block = jnp.where(t < cnt[0, k], block, jnp.zeros_like(block))
            acc[slot[t, k]] += jnp.dot(
                vals[k * tiles_step + t], block, preferred_element_type=F32
            )
    me_x, _ = position()
    per_x = YN * CAP
    line = lax.broadcasted_iota(jnp.int32, (ID_ROWS, LANES), 0)
    for k in range(XN):
        x = lax.rem(me_x + k, XN)
        rows = jnp.zeros_like(line)
        for j in range(per_x):
            total = acc[x * per_x + j].astype(BF16)
            rows = jnp.where(line == j, ids[0, x * per_x + j], rows)
            for h in range(2):
                part = total[:, h * LANES : (h + 1) * LANES]
                outs[h * XN + k][pl.ds(j * BLOCK, BLOCK), :] = part
        outs[k][pl.ds(per_x * BLOCK, ID_ROWS), :] = rows.astype(F32).astype(BF16)


def forward_products(src, slot, cnt, feats, vals, ids):
    rows = YN * CAP * BLOCK
    first = jax.ShapeDtypeStruct((rows + ID_ROWS, LANES), BF16)
    second = jax.ShapeDtypeStruct((rows, LANES), BF16)
    return kernel_call(
        forward_kernel,
        "tile_forward",
        (first,) * XN + (second,) * XN,
        [(SMEM, a) for a in (src, slot, cnt, ids)] + [(VMEM, a) for a in (*feats, vals)],
        FORWARD_MIB,
        vals.size * 4 * LANES,
        [pltpu.VMEM((XN * YN * CAP, BLOCK, 2 * LANES), F32)],
    )


def gather_kernel(blocks_dev, recv, ids, outs):
    _, me_y = position()
    chunk = 64
    for i, out in enumerate(outs):
        y = lax.rem(me_y + i, YN)
        rows = {}
        for k in range(XN):
            for c in range(CAP):
                rows[k, c] = ids[pl.ds(k * YN * CAP + y * CAP + c, 1), :][:, :LANES]
        for start in range(0, BLOCK, chunk):
            totals = [jnp.zeros((chunk, LANES), F32) for _ in range(blocks_dev)]
            for (k, c), row in rows.items():
                spot = pl.multiple_of((y * CAP + c) * BLOCK + start, chunk)
                part = recv[k][pl.ds(spot, chunk), :].astype(F32)
                for b in range(blocks_dev):
                    totals[b] = totals[b] + jnp.where(row == float(b), part, 0.0)
            for b in range(blocks_dev):
                out[pl.ds(b * BLOCK + start, chunk), :] = totals[b].astype(BF16)


def gather0_kernel(blocks_dev, *refs):
    recv, outs, ids = refs[:XN], refs[XN:-1], refs[-1]
    per_x = YN * CAP
    for k in range(XN):
        got = recv[k][pl.ds(per_x * BLOCK, ID_ROWS), :].astype(F32)[:per_x]
        ids[pl.ds(k * per_x, per_x), :] = jnp.concatenate([got, got], axis=1)
    gather_kernel(blocks_dev, recv, ids, outs)


def gather1_kernel(blocks_dev, *refs):
    gather_kernel(blocks_dev, refs[:XN], refs[XN], refs[XN + 1 :])


def gather_blocks(recv, blocks_dev, ids=None):
    outs = (jax.ShapeDtypeStruct((blocks_dev * BLOCK, LANES), BF16),) * YN
    if ids is None:
        outs += (jax.ShapeDtypeStruct((XN * YN * CAP, 2 * LANES), F32),)
    return kernel_call(
        functools.partial(gather0_kernel if ids is None else gather1_kernel, blocks_dev),
        "block_sums",
        outs,
        [(VMEM, a) for a in recv] + ([] if ids is None else [(VMEM, ids)]),
        6,
        GATHER_FLOPS,
    )


def summed(parts):
    total = parts[0][...].astype(F32)
    for part in parts[1:]:
        total = total + part[...].astype(F32)
    return total.astype(BF16)


def half_kernel(*refs):
    refs[-1][...] = summed(refs[:-1])


def half_sum(parts):
    return kernel_call(
        half_kernel,
        "half_sum",
        jax.ShapeDtypeStruct(parts[0].shape, BF16),
        [(VMEM, a) for a in parts],
        4,
        HALF_FLOPS,
    )


def dense_kernel(*refs):
    agg0, parts, (weight, cot, act, grad, wgrad) = refs[0], refs[1 : 1 + YN], refs[1 + YN :]
    agg = jnp.concatenate([agg0[...], summed(parts)], axis=1)
    w = weight[...]
    pre = jnp.dot(agg, w, preferred_element_type=F32)
    sig = 1.0 / (1.0 + jnp.exp(-pre))
    act[...] = (pre * sig).astype(BF16)
    slope = sig * (1.0 + pre * (1.0 - sig))
    pre_grad = (cot[...].astype(F32) * slope).astype(BF16)
    grad[...] = lax.dot_general(
        pre_grad, w, (((1,), (1,)), ((), ())), preferred_element_type=F32
    ).astype(BF16)
    wgrad[...] = lax.dot_general(
        agg, pre_grad, (((0,), (0,)), ((), ())), preferred_element_type=F32
    ).astype(BF16)


def dense(agg0, parts, weight, cot):
    nodes, channels = cot.shape
    full = jax.ShapeDtypeStruct((nodes, channels), BF16)
    return kernel_call(
        dense_kernel,
        "dense_layer",
        (full, full, jax.ShapeDtypeStruct((channels, channels), BF16)),
        [(VMEM, a) for a in (agg0, *parts, weight, cot)],
        10,
        DENSE_FLOPS,
    )


def reply_kernel(ids, g0, r1, r2, r3, own, o1, o2, o3, held, sem):
    _, me_y = position()
    chunk = 32
    for k, grads in enumerate((g0, r1, r2, r3)):
        y = lax.rem(me_y - k + YN, YN)
        rows = {}
        for i in range(XN):
            for c in range(CAP):
                rows[i, c] = ids[pl.ds(i * YN * CAP + y * CAP + c, 1), :]
        for start in range(0, BLOCK, chunk):
            blocks = [grads[b, pl.ds(start, chunk), :].astype(F32) for b in range(grads.shape[0])]
            for (i, c), row in rows.items():
                picked = jnp.where(row == 0.0, blocks[0], 0.0)
                for b in range(1, len(blocks)):
                    picked = jnp.where(row == float(b), blocks[b], picked)
                spot = pl.multiple_of((y * CAP + c) * BLOCK + start, chunk)
                (held, o1, o2, o3)[i][pl.ds(spot, chunk), :] = picked.astype(BF16)
    store = pltpu.make_async_copy(held, own, sem)
    store.start()
    store.wait()


def reply_slots(ids, grads, blocks_dev):
    channels = grads[0].shape[1]
    out = jax.ShapeDtypeStruct((YN * CAP * BLOCK, channels), BF16)
    grads = [g.reshape(blocks_dev, BLOCK, channels) for g in grads]
    return kernel_call(
        reply_kernel,
        "slot_replies",
        (out,) * XN,
        [(VMEM, a) for a in (ids, *grads)],
        6,
        REPLY_FLOPS,
        [pltpu.VMEM(out.shape, BF16), pltpu.SemaphoreType.DMA],
        (HBM,) + (VMEM,) * (XN - 1),
    )


def backward_kernel(
    src, slot, cnt, b0, b1, b2, b3, vals, om2, om1, own, op1, op2, acc, ret, in_sem
):
    per_x = YN * CAP
    me_x, _ = position()
    load = pltpu.make_async_copy(b0, ret.at[pl.ds(me_x * per_x, per_x)], in_sem)
    load.start()
    for k, back in ((1, b1), (2, b2), (3, b3)):
        x = lax.rem(me_x + k, XN)
        for j in range(per_x):
            ret[x * per_x + j] = back[pl.ds(j * BLOCK, BLOCK), :]
    load.wait()
    steps = cnt.shape[1]
    tiles_step = vals.shape[0] // steps
    acc[...] = jnp.zeros_like(acc)
    for k in range(steps):
        for t in range(tiles_step):
            block = ret[slot[t, k]]
            block = jnp.where(t < cnt[0, k], block, jnp.zeros_like(block))
            acc[k, src[t, k]] += lax.dot_general(
                vals[k * tiles_step + t],
                block,
                (((0,), (0,)), ((), ())),
                preferred_element_type=F32,
            )
    for k, out in enumerate((om2, om1, own, op1, op2)):
        for b in range(acc.shape[1]):
            out[pl.ds(b * BLOCK, BLOCK), :] = acc[k, b].astype(BF16)


def backward_products(src, slot, cnt, back, vals, blocks_dev):
    nodes, channels = blocks_dev * BLOCK, back[0].shape[1]
    steps = cnt.shape[1]
    send = jax.ShapeDtypeStruct((nodes, channels), BF16)
    own_back = back[0].reshape(YN * CAP, BLOCK, channels)
    return kernel_call(
        backward_kernel,
        "tile_backward",
        (send,) * 5,
        [(SMEM, a) for a in (src, slot, cnt)]
        + [(HBM, own_back)]
        + [(VMEM, a) for a in (*back[1:], vals)],
        12,
        BACK_FLOPS,
        [
            pltpu.VMEM((steps, blocks_dev, BLOCK, channels), F32),
            pltpu.VMEM((XN * YN * CAP, BLOCK, channels), BF16),
            pltpu.SemaphoreType.DMA,
        ],
    )


def final_kernel(*refs):
    refs[-1][...] = summed(refs[:-1]).astype(BF16)


def final_sum(own, parts):
    return kernel_call(
        final_kernel,
        "grad_sum",
        jax.ShapeDtypeStruct(own.shape, BF16),
        [(VMEM, a) for a in (own, *parts)],
        4,
        FINAL_FLOPS,
    )


def spread_kernel(parts, out):
    total = parts[0].astype(F32)
    for i in range(1, parts.shape[0]):
        total = total + parts[i].astype(F32)
    for i in range(out.shape[0]):
        out[i] = total.astype(out.dtype)


def sum_and_spread(parts, copies, dtype=F32):
    return kernel_call(
        spread_kernel,
        "sum_and_spread",
        jax.ShapeDtypeStruct((copies,) + parts.shape[1:], dtype),
        [(VMEM, parts)],
        2,
        SPREAD_FLOPS,
    )


def weight_piece(local_grad):
    rows, dom = lax.axis_size("rows"), lax.axis_size("dom")
    outer = dom // INNER
    near = [[i * INNER + j for j in range(INNER)] for i in range(outer)]
    far = [[i * INNER + j for i in range(outer)] for j in range(INNER)]
    pieces = local_grad.reshape(rows, local_grad.shape[0] // rows, local_grad.shape[1])
    piece = sum_and_spread(exchange(pieces, "rows"), INNER)
    piece = sum_and_spread(exchange(piece, "dom", near), outer)
    return sum_and_spread(exchange(piece, "dom", far), rows, BF16)


def per_device(
    features, weight, tile_values, tile_source, tile_slot, slot_block, tile_count, cotangent
):
    blocks_dev = features.shape[0] // BLOCK
    channels = features.shape[1]
    vals = tile_values.reshape(-1, BLOCK, BLOCK)
    src, slot = tile_source[0].T, tile_slot[0].T
    cnt = tile_count

    near = [dom_shift(features, -o) for o in OFFSETS]
    feats = [near[0], near[1], features, near[2], near[3]]
    feats = [f.reshape(blocks_dev, BLOCK, channels) for f in feats]
    sent = forward_products(src, slot, cnt, feats, vals, slot_block)
    got0 = [sent[0]] + [x_shift(sent[k], k) for k in range(1, XN)]
    got1 = [sent[XN]] + [x_shift(sent[XN + k], k) for k in range(1, XN)]
    *sums0, ids = gather_blocks(got0, blocks_dev)
    agg0 = half_sum([sums0[0]] + [y_shift(sums0[k], k) for k in range(1, YN)])
    sums1 = gather_blocks(got1, blocks_dev, ids)
    parts = [sums1[0]] + [y_shift(sums1[k], k) for k in range(1, YN)]
    activations, grad, local_grad = dense(agg0, parts, weight, cotangent)

    piece = weight_piece(local_grad)
    grads = [grad] + [y_shift(grad, k) for k in range(1, YN)]
    reply = reply_slots(ids, grads, blocks_dev)
    back = [reply[0]] + [None] * (XN - 1)
    for k in (1, 3, 2):
        back[k] = x_shift(reply[k], -k)
    terms = list(backward_products(src, slot, cnt, back, vals, blocks_dev))
    own = terms.pop(HALF)
    terms = [dom_shift(t, o) for t, o in zip(terms, OFFSETS)]
    weight_grad = exchange(piece, "rows").reshape(local_grad.shape).astype(F32)
    feature_grad = final_sum(own, terms)
    return (activations, feature_grad, weight_grad)


def solution(mesh):
    return jax.shard_map(
        per_device,
        mesh=mesh,
        in_specs=(
            P(("dom", "rows"), None),
            P(),
            P(("dom", "rows"), None, None, None, None),
            P(("dom", "rows"), None, None),
            P(("dom", "rows"), None, None),
            P(("dom", "rows"), None),
            P(("dom", "rows"), None),
            P(("dom", "rows"), None),
        ),
        out_specs=(P(("dom", "rows"), None), P(("dom", "rows"), None), P()),
        check_vma=False,
    )
```
